256 devices in a mesh: section: 2 (over core), wide: 32 (over z_lo, y, x), narrow: 4 (over z_hi).
Axes of the slice: x: 4, y: 4, z: 8 (z_hi: 4, z_lo: 2; z = z_hi * 2 + z_lo), core: 2. Of those that a mesh axis runs over, the one named last changes fastest.
Arguments:
- teacher_rows: bfloat16 [24576, 6656], P(('section', 'wide'), 'narrow'), may hold values from -150 to 150, as said below
- teacher_gain: bfloat16 [6656], P('narrow'), may hold values from 0.5 to 1.5
- projector: bfloat16 [6656, 3072], P('narrow', 'wide'), may hold values from -0.078125 to 0.078125
- student_rows: bfloat16 [24576, 3072], P(('section', 'wide'), 'narrow'), may hold values from -16 to 16
- student_weight: bfloat16 [3072, 3072], P(None, 'narrow'), may hold values from -0.109375 to 0.109375
Outputs:
- input_grad: bfloat16 [24576, 3072], P(('section', 'wide'), 'narrow')
- weight_grad: float32 [3072, 3072], P(('section', 'wide'), 'narrow')
The draws below stay inside these ranges and needn't reach their ends.
Inputs may be any that keep to these rules, and one draw needn't show every extreme that they name: teacher_rows have row scales and feature scales that differ.
All inputs are finite; a program needn't handle non-finite values.
Results may differ from the reference program's by a relative error of at most 0.015.
Values may be sent and summed in bfloat16 or wider, within the bound.
A program may use at most 128 MiB of HBM per device.

```python
import jax
import jax.numpy as jnp
from jax import lax

DT = 6656
DS = 3072
TOKENS = 24576
N_NARROW = 4


def draw_teacher_rows(key, part):
    key = jax.random.fold_in(key, 11)
    first_key, second_key = jax.random.split(key, 2)
    position = jnp.arange(DT, dtype=jnp.float32) / DT
    column_scale = jnp.exp(jnp.log(3.0) * position)[None, :]
    row_scale = jnp.exp(jax.random.uniform(first_key, (TOKENS, 1), minval=0.0, maxval=jnp.log(10.0)))
    base_values = jnp.clip(jax.random.normal(second_key, (TOKENS, DT)), -5.0, 5.0)
    return (base_values * column_scale * row_scale).astype(jnp.bfloat16)


def raised(values, rng, source, target, blocks, factor):
    owner, partner = [(jnp.arange(values.shape[dim]) // (values.shape[dim] // blocks)).reshape([-1 if axis == dim else 1 for axis in range(values.ndim)]) for dim in (source, target)]
    chosen = jax.random.permutation(rng, blocks)[partner]
    strong = (owner == chosen) | (owner == (partner + blocks // 2) % blocks)
    return jnp.where(strong, factor * values, values)


def shard_levels(rng, shape, shards, least, high):
    def one(axis_at, blocks):
        heights = jax.random.uniform(jax.random.fold_in(jax.random.fold_in(rng, 6), axis_at), (blocks,), jnp.float32, least / len(shards), high / len(shards))
        return jnp.repeat(jnp.exp(heights), shape[axis_at] // blocks).reshape((-1,) + (1,) * (len(shape) - axis_at - 1))

    level = one(*shards[0])
    for cut in shards[1:]:
        level = level * one(*cut)
    return level


def normal_values(rng, extent, spread, bound, cuts=(), kind=jnp.bfloat16):
    values = jax.random.normal(rng, extent, jnp.float32) * spread
    if len(cuts) > 0:
        values = shard_levels(rng, extent, cuts, -0.22, 0.18) * values
    return jnp.clip(values, min=-bound, max=bound).astype(kind)


def noise_with(own_key, shape, scale, reach, cuts, heavy, kind=jnp.bfloat16):
    entries = scale * jax.random.normal(own_key, shape, jnp.float32)
    if cuts:
        entries = entries * shard_levels(own_key, shape, cuts, -0.22, 0.18)
    return jnp.clip(raised(entries, jax.random.fold_in(own_key, 3), *heavy), -reach, reach).astype(kind)


def setup_inputs(seed: int = 0) -> dict:
    keys = jax.random.split(jax.random.key(seed), 6)
    teacher_rows = draw_teacher_rows(jax.random.fold_in(keys[5], 71), 0)
    teacher_gain = jnp.clip(1.0 + 0.1 * jax.random.normal(keys[1], (DT,), jnp.float32), 0.5, 1.5).astype(jnp.bfloat16)
    projector = normal_values(keys[2], (DT, DS), DT ** -0.5, 0.078125, ((0, 4), (1, 32)))
    student_rows = noise_with(keys[3], (TOKENS, DS), 1.0, 16.0, ((0, 64), (1, 4)), (0, 1, 64, 4.0))
    student_weight = normal_values(keys[4], (DS, DS), DS ** -0.5, 0.109375, ((1, 4),))
    return {"teacher_rows": teacher_rows, "teacher_gain": teacher_gain, "projector": projector, "student_rows": student_rows, "student_weight": student_weight}


def reference(teacher_rows, teacher_gain, projector, student_rows, student_weight):
    teacher_f32 = teacher_rows.astype(jnp.float32)
    mean_square = lax.optimization_barrier(jnp.mean(teacher_f32 * teacher_f32, axis=1, keepdims=True))
    hidden = (teacher_f32 * lax.rsqrt(mean_square + 1e-05) * teacher_gain.astype(jnp.float32)[None, :]).astype(jnp.bfloat16)
    paired = jnp.roll(hidden, -(TOKENS // 2), axis=0)
    quarter_width = DT // N_NARROW
    target = jnp.zeros((TOKENS, DS), jnp.float32)
    for quarter in range(N_NARROW):
        lower = quarter * quarter_width
        partial_value = jnp.dot(paired[:, lower:lower + quarter_width], projector[lower:lower + quarter_width, :], preferred_element_type=jnp.float32).astype(jnp.bfloat16)
        target = target + partial_value.astype(jnp.float32)
    target = target.astype(jnp.bfloat16)
    output = student_rows.astype(jnp.float32) + jnp.dot(student_rows, student_weight, preferred_element_type=jnp.float32)
    mismatch = (output - target.astype(jnp.float32)).astype(jnp.bfloat16)
    student_width = DS // N_NARROW
    back_total = jnp.zeros((TOKENS, DS), jnp.float32)
    for quarter in range(N_NARROW):
        lower = quarter * student_width
        back_part = jnp.dot(mismatch[:, lower:lower + student_width], student_weight[:, lower:lower + student_width].T, preferred_element_type=jnp.float32).astype(jnp.bfloat16)
        back_total = back_total + back_part.astype(jnp.float32)
    input_grad = (mismatch.astype(jnp.float32) + back_total).astype(jnp.bfloat16)
    weight_grad = jnp.dot(student_rows.T, mismatch, preferred_element_type=jnp.float32) / jnp.sqrt(jnp.float32(TOKENS))
    return (input_grad, weight_grad)
```

```python
import functools

import jax
import jax.numpy as jnp
from jax import lax
from jax.experimental import pallas as pl
from jax.experimental.pallas import tpu as pltpu
from jax.sharding import PartitionSpec as P

MESH = pl.DeviceIdType.MESH
F32 = jnp.float32
BF16 = jnp.bfloat16

GATHER = 0
ZSWAP = 40
WSEND = 41
WRECV = 44
SQUARES = 45
PAIRED = 48
SIBLING = 49
NARROW_RS = 50
NARROW_AG = 56
CORE_SUM = 62
WIDE_RS = 66
ZSUM = 90
FINAL = 91
SLOTS = 92


class Ring:
    def __init__(self, copy, base, out, opp_in, left_in, right_in, right, left):
        self.out, self.opp_in, self.left_in, self.right_in = out, opp_in, left_in, right_in
        self.copies = [
            copy(out.at[0, 0], opp_in.at[0], base + 0, right),
            copy(out.at[0, 1], opp_in.at[1], base + 1, left),
            copy(out.at[1, 1], left_in.at[1], base + 2, right),
            copy(out.at[2, 0], right_in.at[0], base + 3, left),
            copy(out.at[1, 0], left_in.at[0], base + 4, right),
            copy(out.at[2, 1], right_in.at[1], base + 5, left),
        ]

    def send_far(self, load):
        for h in range(2):
            self.out[0, h] = load(h).astype(BF16)
            self.copies[h].start()

    def send_right_early(self, load):
        self.out[1, 1] = load(1).astype(BF16)
        self.copies[2].start()

    def send_left_early(self, load):
        self.out[2, 0] = load(0).astype(BF16)
        self.copies[3].start()

    def send_right_late(self, load):
        self.copies[0].wait_recv()
        self.out[1, 0] = (load(0) + self.opp_in[0].astype(F32)).astype(BF16)
        self.copies[4].start()

    def send_left_late(self, load):
        self.copies[1].wait_recv()
        self.out[2, 1] = (load(1) + self.opp_in[1].astype(F32)).astype(BF16)
        self.copies[5].start()

    def wait_half(self, h):
        if h == 0:
            self.copies[3].wait_recv()
            self.copies[4].wait_recv()
        else:
            self.copies[2].wait_recv()
            self.copies[5].wait_recv()

    def received(self, h):
        return self.left_in[h].astype(F32) + self.right_in[h].astype(F32)

    def wait_sends(self):
        for item in self.copies:
            item.wait_send()


def kernel(
    t_ref, g_ref, pt_ref, wt_ref, x_ref, xt_ref, ig_ref, wg_ref,
    ct, lhs, hid, sq, part, n_out, n_opp, n_left, n_right, m, igacc,
    gk, core_out, core_in, w_out, w_opp, w_left, w_right, hk, v_out, v_opp, v_left, v_right,
    res, z_out, z_in, fin, send_sem, recv_sem, local_sem,
):
    c = lax.axis_index("section")
    w = lax.axis_index("wide")
    n = lax.axis_index("narrow")
    x, y, zl = w % 4, (w // 4) % 4, w // 16
    tokens, kt = t_ref.shape
    ks = x_ref.shape[1]
    half = pt_ref.shape[0] // 2
    depth = kt + ks
    cut = (depth // 256 + 1) * 128
    cols = ks // 2
    rows = pl.ds(pl.multiple_of(half * c, half), half)

    def at(zz, yy, xx):
        return zz * 16 + yy * 4 + xx

    sibling = {"section": 1 - c}
    x_next, x_prev = {"wide": at(zl, y, (x + 1) % 4)}, {"wide": at(zl, y, (x + 3) % 4)}
    y_next, y_prev = {"wide": at(zl, (y + 1) % 4, x)}, {"wide": at(zl, (y + 3) % 4, x)}
    z_other = {"wide": at(1 - zl, y, x)}
    n_dev = [None] + [{"narrow": (n + d) % 4} for d in (1, 2, 3)]

    target_id = {"section": n // 2, "wide": at(n % 2, y, x), "narrow": (n + 2 * zl + c) % 4}
    own_piece = jnp.logical_and(n == 2 * c + zl, 2 * zl + c == 0)
    from_row = 2 * c + zl
    offset = (n - from_row + 4) % 4
    source_id = {"section": offset % 2, "wide": at(offset // 2, y, x), "narrow": from_row}

    barrier = pltpu.get_barrier_semaphore()
    greeted = [sibling, x_next, x_prev, y_next, y_prev, z_other, n_dev[1], n_dev[2], n_dev[3]]
    for device in greeted:
        pl.semaphore_signal(barrier, inc=1, device_id=device, device_id_type=MESH)

    @pl.when(jnp.logical_not(own_piece))
    def _():
        pl.semaphore_signal(barrier, inc=1, device_id=source_id, device_id_type=MESH)

    pl.semaphore_wait(barrier, jnp.where(own_piece, len(greeted), len(greeted) + 1))

    def copy(src, dst, slot, device):
        return pltpu.make_async_remote_copy(
            src_ref=src, dst_ref=dst, send_sem=send_sem.at[slot], recv_sem=recv_sem.at[slot],
            device_id=device, device_id_type=MESH,
        )

    w_cols = pl.ds(kt, ks)
    w_home = ct.at[w, rows, w_cols]
    owner = w // 8
    w_copies = [
        pltpu.make_async_remote_copy(
            src_ref=wt_ref.at[(n + d) % 4], dst_ref=w_home, send_sem=send_sem.at[WSEND + d - 1],
            recv_sem=recv_sem.at[WRECV], device_id=n_dev[d], device_id_type=MESH,
        )
        for d in (1, 2, 3)
    ]

    @pl.when(n == owner)
    def _():
        for item in w_copies:
            item.start()
        ct[w, rows, w_cols] = wt_ref[n]

    ct[w, rows, pl.ds(0, kt)] = pt_ref[rows, :]

    eye = lax.broadcasted_iota(jnp.int32, (128, 128), 0) == lax.broadcasted_iota(jnp.int32, (128, 128), 1)
    groups = tokens // 128
    sq[0] = jnp.zeros((8, 128), F32)
    for i in range(groups):
        part_t = t_ref[128 * i : 128 * i + 128, :].astype(F32)
        col = jnp.sum(part_t * part_t, axis=1, keepdims=True)
        sq[0, i : i + 1, :] = jnp.sum(jnp.where(eye, col, 0.0), axis=0, keepdims=True)
    sq_copies = [copy(sq.at[0], sq.at[d], SQUARES + d - 1, n_dev[d]) for d in (1, 2, 3)]
    for item in sq_copies:
        item.start()

    @pl.when(n != owner)
    def _():
        w_copies[0].wait_recv()

    def slab(index, part=None):
        if part is None:
            return ct.at[index, rows]
        return ct.at[index, rows, pl.ds(0, cut) if part == 0 else pl.ds(cut, depth - cut)]

    def spread(index, slot, device, part=None):
        return copy(slab(index, part), slab(index, part), slot, device)

    sent = []

    def go(item):
        item.start()
        sent.append(item)

    def to_sibling(index):
        copy(slab(index), slab(index), SIBLING, sibling).start()

    class Family:
        def __init__(self, f):
            self.base = GATHER + 20 * f
            self.f = f
            self.plane = zl if f == 0 else 1 - zl
            self.a, self.b = (x, y) if f == 0 else (y, x)
            self.first = (x_next, x_prev) if f == 0 else (y_next, y_prev)
            self.second = (y_next, y_prev) if f == 0 else (x_next, x_prev)

        def index(self, da, db):
            a, b = (self.a + da) % 4, (self.b + db) % 4
            return at(self.plane, b, a) if self.f == 0 else at(self.plane, a, b)

        def begin(self):
            own = self.index(0, 0)
            go(spread(own, self.base, self.first[0]))
            go(spread(own, self.base + 1, self.first[1]))
            self.second_send(0)
            to_sibling(own)

        ALONG = (0, 3, 1, 2)

        def second_send(self, j):
            index = self.index(self.ALONG[j], 0)
            go(spread(index, self.base + 4 + 4 * j, self.second[0]))
            go(spread(index, self.base + 5 + 4 * j, self.second[1]))

        def first_near(self):
            for side in range(2):
                index = self.index(self.ALONG[1 + side], 0)
                spread(index, self.base + side, self.first[side]).wait_recv()
                go(spread(index, self.base + 2 + side, self.first[side], side))
                self.second_send(1 + side)
                to_sibling(index)

        def first_far(self):
            index = self.index(2, 0)
            for side in range(2):
                spread(index, self.base + 2 + side, self.first[side], side).wait_recv()
            self.second_send(3)
            to_sibling(index)

        def second_near(self, j):
            slot = self.base + 4 + 4 * j
            for side in range(2):
                index = self.index(self.ALONG[j], 3 if side == 0 else 1)
                spread(index, slot + side, self.second[side]).wait_recv()
                go(spread(index, slot + 2 + side, self.second[side], side))
                to_sibling(index)

        def second_far(self, j):
            slot = self.base + 4 + 4 * j
            index = self.index(self.ALONG[j], 2)
            for side in range(2):
                spread(index, slot + 2 + side, self.second[side], side).wait_recv()
            to_sibling(index)

    fams = [Family(0), Family(1)]
    z_copy = spread(w, ZSWAP, z_other)
    go(z_copy)
    fams[0].begin()

    lhs[:, kt:] = x_ref[...]
    for item in sq_copies:
        item.wait_recv()
    inverse = lax.rsqrt((sq[0] + sq[1] + sq[2] + sq[3]) / (4 * kt) + 1e-05)
    gain = g_ref[...].astype(F32)
    for i in range(groups):
        col = jnp.sum(jnp.where(eye, inverse[i : i + 1, :], 0.0), axis=1, keepdims=True)
        span = slice(128 * i, 128 * i + 128)
        hid[span, :] = -(t_ref[span, :].astype(F32) * col * gain).astype(BF16)
    paired_copy = copy(hid, lhs.at[:, pl.ds(0, kt)], PAIRED, sibling)
    go(paired_copy)

    z_copy.wait_recv()
    fams[1].begin()
    for fam in fams:
        fam.first_near()
    for fam in fams:
        fam.second_near(0)
    for fam in fams:
        fam.first_far()
    for j in (1, 2, 3):
        for fam in fams:
            fam.second_near(j)
            fam.second_far(j - 1)
    for fam in fams:
        fam.second_far(3)
    all_half = ct.at[:, rows]
    sibling_all = copy(all_half, all_half, SIBLING, sibling)
    sibling_all.wait_recv()
    paired_copy.wait_recv()

    ring = Ring(copy, NARROW_RS, n_out, n_opp, n_left, n_right, n_dev[1], n_dev[3])

    def product(i, carry):
        r, h = i // 2, i % 2
        d = jnp.where(r == 0, 2, jnp.where(r == 1, 1, jnp.where(r == 2, 3, 0)))
        b = (n + d) % 4
        block = ct[pl.ds(8 * b + 4 * h, 4)].reshape(cols, depth)
        part[r, h] = lax.dot_general(
            lhs[...], block, (((1,), (1,)), ((), ())), preferred_element_type=F32
        )

        @pl.when(i == 1)
        def _():
            ring.send_far(lambda k: part[0, k])

        @pl.when(i == 3)
        def _():
            ring.send_right_early(lambda k: part[1, k])

        @pl.when(i == 5)
        def _():
            ring.send_left_early(lambda k: part[2, k])

        return carry

    lax.fori_loop(0, 8, product, 0)
    ring.send_right_late(lambda k: part[1, k])
    ring.send_left_late(lambda k: part[2, k])

    ag = [
        copy(m.at[n, 0], m.at[n, 0], NARROW_AG, n_dev[1]),
        copy(m.at[n, 1], m.at[n, 1], NARROW_AG + 1, n_dev[1]),
        copy(m.at[n, 0], m.at[n, 0], NARROW_AG + 2, n_dev[3]),
        copy(m.at[n, 1], m.at[n, 1], NARROW_AG + 3, n_dev[3]),
        copy(m.at[(n + 3) % 4, 0], m.at[(n + 3) % 4, 0], NARROW_AG + 4, n_dev[1]),
        copy(m.at[(n + 1) % 4, 1], m.at[(n + 1) % 4, 1], NARROW_AG + 5, n_dev[3]),
    ]
    for h in range(2):
        ring.wait_half(h)
        own = part[3, h] + x_ref[:, cols * h : cols * h + cols].astype(F32)
        m[n, h] = (own + ring.received(h)).astype(BF16)
        ag[h].start()
        ag[2 + h].start()

    igacc[...] = jnp.zeros((tokens, ks), F32)

    def core_copy(f, h):
        return copy(core_out.at[f, h], core_in.at[f, h], CORE_SUM + 2 * f + h, sibling)

    def backward(i, carry):
        r, h = i // 2, i % 2

        @pl.when(i == 2)
        def _():
            ag[0].wait_recv()
            ag[4].start()
            ag[3].wait_recv()
            ag[5].start()
            ag[1].wait_recv()

        @pl.when(i == 4)
        def _():
            ag[2].wait_recv()

        @pl.when(i == 6)
        def _():
            ag[4].wait_recv()
            ag[5].wait_recv()

        d = jnp.where(r == 0, 0, jnp.where(r == 1, 3, jnp.where(r == 2, 1, 2)))
        b = (n + d) % 4
        f = d // 2
        piece = m[b, h]
        block = ct[pl.ds(8 * b + 4 * h, 4), :, pl.ds(kt, ks)].reshape(cols, ks)
        igacc[...] += jnp.dot(piece, block, preferred_element_type=F32)
        grad = jnp.dot(xt_ref[...], piece, preferred_element_type=F32)

        @pl.when(c == d % 2)
        def _():
            gk[f, h] = grad.reshape(4, 4, half, cols)

        @pl.when(c != d % 2)
        def _():
            core_out[f, h] = grad.astype(BF16).reshape(4, 4, half, cols)
            core_copy(f, h).start()

        return carry

    lax.fori_loop(0, 8, backward, 0)
    for h in range(2):
        span = slice(cols * h, cols * h + cols)
        ig_ref[:, span] = (m[n, h].astype(F32) + igacc[:, span]).astype(BF16)

    for f in range(2):
        for h in range(2):
            core_copy(f, h).wait_recv()
            gk[f, h] += core_in[f, h].astype(F32)

    ring1, ring2 = [], []
    for f in range(2):
        first = (x_next, x_prev) if f == 0 else (y_next, y_prev)
        second = (y_next, y_prev) if f == 0 else (x_next, x_prev)
        ring1.append(
            Ring(copy, WIDE_RS + 6 * f, w_out.at[f], w_opp.at[f], w_left.at[f], w_right.at[f], *first)
        )
        ring2.append(
            Ring(copy, WIDE_RS + 12 + 6 * f, v_out.at[f], v_opp.at[f], v_left.at[f], v_right.at[f], *second)
        )

    def outer(f, da):
        if f == 0:
            return lambda h: gk[0, h, :, (x + da) % 4]
        return lambda h: gk[1, h, (y + da) % 4]

    def inner(f, db):
        mine = y if f == 0 else x
        return lambda h: hk[f, h, (mine + db) % 4]

    for rings, load in ((ring1, outer), (ring2, inner)):
        for f in range(2):
            rings[f].send_far(load(f, 2))
        for f in range(2):
            rings[f].send_right_early(load(f, 1))
            rings[f].send_left_early(load(f, 3))
        for f in range(2):
            rings[f].send_right_late(load(f, 1))
            rings[f].send_left_late(load(f, 3))
        for f in range(2):
            for h in range(2):
                rings[f].wait_half(h)
                total = load(f, 0)(h) + rings[f].received(h)
                if rings is ring1:
                    hk[f, h] = total
                else:
                    res[f, h] = total

    z_out[...] = res[1 - zl].astype(BF16)
    z_sum = copy(z_out, z_in, ZSUM, z_other)
    z_sum.start()
    z_sum.wait_recv()
    scale = 1.0 / (tokens * 64.0) ** 0.5
    for h in range(2):
        fin[:, cols * h : cols * h + cols] = (res[zl, h] + z_in[h].astype(F32)) * scale
    final = copy(fin, wg_ref, FINAL, target_id)

    @pl.when(own_piece)
    def _():
        local = pltpu.make_async_copy(fin, wg_ref, local_sem)
        local.start()
        local.wait()

    @pl.when(jnp.logical_not(own_piece))
    def _():
        final.start()
        final.wait_recv()
        final.wait_send()

    z_sum.wait_send()
    for item in sent + sq_copies + ag:
        item.wait_send()
    sibling_all.wait_send()
    ring.wait_sends()
    for one in ring1 + ring2:
        one.wait_sends()
    for f in range(2):
        for h in range(2):
            core_copy(f, h).wait_send()

    @pl.when(n == owner)
    def _():
        for item in w_copies:
            item.wait_send()


def shards(teacher_rows, teacher_gain, projector, student_rows, student_weight):
    tokens, kt = teacher_rows.shape
    ks = student_rows.shape[1]
    width = projector.shape[1]
    half, cols, depth = width // 2, ks // 2, kt + ks
    c, w = lax.axis_index("section"), lax.axis_index("wide")
    weight_cols = lax.dynamic_slice(student_weight, (0, width * (w % 8) + half * c), (4 * ks, half))
    weight_t = weight_cols.reshape(4, ks, half).transpose(0, 2, 1)
    vmem = pl.BlockSpec(memory_space=pltpu.VMEM)
    return pl.pallas_call(
        kernel,
        out_shape=(
            jax.ShapeDtypeStruct((tokens, ks), BF16),
            jax.ShapeDtypeStruct((half, ks), F32),
        ),
        in_specs=[vmem] * 6,
        out_specs=(vmem, vmem),
        scratch_shapes=[
            pltpu.VMEM((32, width, depth), BF16),
            pltpu.VMEM((tokens, depth), BF16),
            pltpu.VMEM((tokens, kt), BF16),
            pltpu.VMEM((4, 8, 128), F32),
            pltpu.VMEM((4, 2, tokens, cols), F32),
            pltpu.VMEM((3, 2, tokens, cols), BF16),
            pltpu.VMEM((2, tokens, cols), BF16),
            pltpu.VMEM((2, tokens, cols), BF16),
            pltpu.VMEM((2, tokens, cols), BF16),
            pltpu.VMEM((4, 2, tokens, cols), BF16),
            pltpu.VMEM((tokens, ks), F32),
            pltpu.VMEM((2, 2, 4, 4, half, cols), F32),
            pltpu.VMEM((2, 2, 4, 4, half, cols), BF16),
            pltpu.VMEM((2, 2, 4, 4, half, cols), BF16),
            pltpu.VMEM((2, 3, 2, 4, half, cols), BF16),
            pltpu.VMEM((2, 2, 4, half, cols), BF16),
            pltpu.VMEM((2, 2, 4, half, cols), BF16),
            pltpu.VMEM((2, 2, 4, half, cols), BF16),
            pltpu.VMEM((2, 2, 4, half, cols), F32),
            pltpu.VMEM((2, 3, 2, half, cols), BF16),
            pltpu.VMEM((2, 2, half, cols), BF16),
            pltpu.VMEM((2, 2, half, cols), BF16),
            pltpu.VMEM((2, 2, half, cols), BF16),
            pltpu.VMEM((2, 2, half, cols), F32),
            pltpu.VMEM((2, half, cols), BF16),
            pltpu.VMEM((2, half, cols), BF16),
            pltpu.VMEM((half, ks), F32),
            pltpu.SemaphoreType.DMA((SLOTS,)),
            pltpu.SemaphoreType.DMA((SLOTS,)),
            pltpu.SemaphoreType.DMA,
        ],
        compiler_params=pltpu.CompilerParams(
            collective_id=0, has_side_effects=True, vmem_limit_bytes=60 * 2**20
        ),
    )(
        teacher_rows,
        teacher_gain.reshape(1, kt),
        projector.T,
        weight_t,
        student_rows,
        student_rows.T,
    )


def solution(mesh):
    placed = (
        P(("section", "wide"), "narrow"),
        P("narrow"),
        P("narrow", "wide"),
        P(("section", "wide"), "narrow"),
        P(None, "narrow"),
    )
    return jax.shard_map(
        shards,
        mesh=mesh,
        in_specs=placed,
        out_specs=(P(("section", "wide"), "narrow"), P(("section", "wide"), "narrow")),
        check_vma=False,
    )
```

```python
import functools

import jax
import jax.numpy as jnp
from jax import lax
from jax.experimental import pallas as pl
from jax.experimental.pallas import tpu as pltpu
from jax.sharding import PartitionSpec as P

MESH = pl.DeviceIdType.MESH
F32 = jnp.float32
BF16 = jnp.bfloat16

GATHER = 0
ZSWAP = 40
WSEND = 41
WRECV = 44
SQUARES = 45
PAIRED = 48
SIBLING = 49
NARROW_RS = 51
NARROW_AG = 57
CORE_SUM = 63
WIDE_RS = 67
FINAL = 71
SLOTS = 75


def kernel(
    t_ref, g_ref, pt_ref, wt_ref, x_ref, xt_ref, ig_ref, wg_ref,
    ct, lhs, hid, sq, part, far_out, near_out, far_in, near_in, m, igacc,
    kept, core_out, core_in, wide_out, wide_in, fin_out, fin_in, send_sem, recv_sem,
):
    c = lax.axis_index("section")
    w = lax.axis_index("wide")
    n = lax.axis_index("narrow")
    x, y, zl = w % 4, (w // 4) % 4, w // 16
    tokens, kt = t_ref.shape
    ks = x_ref.shape[1]
    half = pt_ref.shape[0] // 2
    depth = kt + ks
    cut = (depth // 256 + 1) * 128
    cols = ks // 2
    rows = pl.ds(pl.multiple_of(half * c, half), half)

    def at(zz, yy, xx):
        return zz * 16 + yy * 4 + xx

    sibling = {"section": 1 - c}
    z_other = {"wide": at(1 - zl, y, x)}
    n_dev = [None] + [{"narrow": (n + d) % 4} for d in (1, 2, 3)]

    def peer(k):
        return (y + k // 4) % 4, (x + k % 4) % 4

    def target(d):
        return {"section": n // 2, "wide": at(n % 2, y, x), "narrow": (n + d) % 4}

    at_home = n == 2 * c + zl
    sources = [
        ({"section": cc, "wide": at(zz, y, x), "narrow": 2 * c + zl}, jnp.logical_and(at_home, jnp.logical_and(cc == c, zz == zl)))
        for zz in range(2)
        for cc in range(2)
    ]

    barrier = pltpu.get_barrier_semaphore()
    greeted = [sibling, z_other, n_dev[1], n_dev[2], n_dev[3]]
    for device in greeted:
        pl.semaphore_signal(barrier, inc=1, device_id=device, device_id_type=MESH)

    def greet(k, carry):
        yy, xx = peer(k)
        pl.semaphore_signal(barrier, inc=1, device_id={"wide": at(zl, yy, xx)}, device_id_type=MESH)
        return carry

    lax.fori_loop(1, 16, greet, 0)
    for device, mine in sources:

        @pl.when(jnp.logical_not(mine))
        def _():
            pl.semaphore_signal(barrier, inc=1, device_id=device, device_id_type=MESH)

    pl.semaphore_wait(barrier, jnp.where(at_home, len(greeted) + 18, len(greeted) + 19))

    def copy(src, dst, slot, device):
        return pltpu.make_async_remote_copy(
            src_ref=src, dst_ref=dst, send_sem=send_sem.at[slot], recv_sem=recv_sem.at[slot],
            device_id=device, device_id_type=MESH,
        )

    w_cols = pl.ds(kt, ks)
    w_home = ct.at[w, rows, w_cols]
    owner = w // 8
    w_copies = [
        pltpu.make_async_remote_copy(
            src_ref=wt_ref.at[(n + d) % 4], dst_ref=w_home, send_sem=send_sem.at[WSEND + d - 1],
            recv_sem=recv_sem.at[WRECV], device_id=n_dev[d], device_id_type=MESH,
        )
        for d in (1, 2, 3)
    ]

    @pl.when(n == owner)
    def _():
        for item in w_copies:
            item.start()
        ct[w, rows, w_cols] = wt_ref[n]

    ct[w, rows, pl.ds(0, kt)] = pt_ref[rows, :]

    eye = lax.broadcasted_iota(jnp.int32, (128, 128), 0) == lax.broadcasted_iota(jnp.int32, (128, 128), 1)
    groups = tokens // 128
    sq[0] = jnp.zeros((8, 128), F32)
    for i in range(groups):
        part_t = t_ref[128 * i : 128 * i + 128, :].astype(F32)
        col = jnp.sum(part_t * part_t, axis=1, keepdims=True)
        sq[0, i : i + 1, :] = jnp.sum(jnp.where(eye, col, 0.0), axis=0, keepdims=True)
    sq_copies = [copy(sq.at[0], sq.at[d], SQUARES + d - 1, n_dev[d]) for d in (1, 2, 3)]
    for item in sq_copies:
        item.start()

    @pl.when(n != owner)
    def _():
        w_copies[0].wait_recv()

    def slab(index, part=None):
        if part is None:
            return ct.at[index, rows]
        return ct.at[index, rows, pl.ds(0, cut) if part == 0 else pl.ds(cut, depth - cut)]

    def spread(index, slot, device, part=None):
        return copy(slab(index, part), slab(index, part), slot, device)

    sent = []

    def go(item):
        item.start()
        sent.append(item)

    along_a, along_b = jnp.where(c == 0, x, y), jnp.where(c == 0, y, x)

    def cell(plane, da, db):
        a, b = (along_a + da) % 4, (along_b + db) % 4
        return plane * 16 + jnp.where(c == 0, 4 * b + a, 4 * a + b)

    first = [{"wide": cell(zl, 1, 0)}, {"wide": cell(zl, 3, 0)}]
    second = [{"wide": cell(zl, 0, 1)}, {"wide": cell(zl, 0, 3)}]
    ALONG = (0, 3, 1, 2)

    class Plane:
        def __init__(self, p, plane):
            self.base, self.p, self.plane = GATHER + 20 * p, p, plane

        def to_sibling(self, index):
            copy(slab(index), slab(index), SIBLING + self.p, sibling).start()

        def whole(self):
            planes = ct.at[pl.ds(16 * self.plane, 16), rows]
            return copy(planes, planes, SIBLING + self.p, sibling)

        def begin(self):
            own = cell(self.plane, 0, 0)
            for side in range(2):
                go(spread(own, self.base + side, first[side]))
            self.second_send(0)
            self.to_sibling(own)

        def second_send(self, j):
            index = cell(self.plane, ALONG[j], 0)
            for side in range(2):
                go(spread(index, self.base + 4 + 4 * j + side, second[side]))

        def first_near(self):
            for side in range(2):
                index = cell(self.plane, ALONG[1 + side], 0)
                spread(index, self.base + side, first[side]).wait_recv()
                go(spread(index, self.base + 2 + side, first[side], side))
                self.second_send(1 + side)
                self.to_sibling(index)

        def first_far(self):
            index = cell(self.plane, 2, 0)
            for side in range(2):
                spread(index, self.base + 2 + side, first[side], side).wait_recv()
            self.second_send(3)
            self.to_sibling(index)

        def second_near(self, j):
            slot = self.base + 4 + 4 * j
            for side in range(2):
                index = cell(self.plane, ALONG[j], 3 if side == 0 else 1)
                spread(index, slot + side, second[side]).wait_recv()
                go(spread(index, slot + 2 + side, second[side], side))
                self.to_sibling(index)

        def second_far(self, j):
            slot = self.base + 4 + 4 * j
            index = cell(self.plane, ALONG[j], 2)
            for side in range(2):
                spread(index, slot + 2 + side, second[side], side).wait_recv()
            self.to_sibling(index)

    p_first = 1 - n // 2
    near_plane, far_plane = Plane(0, p_first), Plane(1, 1 - p_first)
    z_copy = spread(w, ZSWAP, z_other)
    go(z_copy)

    @pl.when(zl != p_first)
    def _():
        z_copy.wait_recv()

    near_plane.begin()

    lhs[:, kt:] = x_ref[...]
    for item in sq_copies:
        item.wait_recv()
    inverse = lax.rsqrt((sq[0] + sq[1] + sq[2] + sq[3]) / (4 * kt) + 1e-05)
    gain = g_ref[...].astype(F32)
    for i in range(groups):
        col = jnp.sum(jnp.where(eye, inverse[i : i + 1, :], 0.0), axis=1, keepdims=True)
        span = slice(128 * i, 128 * i + 128)
        hid[span, :] = -(t_ref[span, :].astype(F32) * col * gain).astype(BF16)
    paired_copy = copy(hid, lhs.at[:, pl.ds(0, kt)], PAIRED, sibling)
    go(paired_copy)

    near_plane.first_near()
    near_plane.second_near(0)
    near_plane.first_far()
    near_plane.second_near(1)
    near_plane.second_far(0)
    near_plane.second_near(2)
    near_plane.second_far(1)
    near_plane.second_near(3)

    @pl.when(zl == p_first)
    def _():
        z_copy.wait_recv()

    far_plane.begin()
    near_plane.second_far(2)
    near_plane.second_far(3)
    paired_copy.wait_recv()
    near_plane.whole().wait_recv()

    e2 = n % 2
    e1 = 1 - e2

    def by(e):
        return {"narrow": (n + 1 + 2 * e) % 4}

    def far_copy(e):
        return copy(far_out.at[e], far_in.at[e], NARROW_RS + e, by(e))

    def early_copy(e):
        return copy(near_out.at[e, 1 - e], near_in.at[e, 1 - e], NARROW_RS + 2 + e, by(e))

    def late_copy(e):
        return copy(near_out.at[e, e], near_in.at[e, e], NARROW_RS + 4 + e, by(e))

    def product(b, h):
        block = ct[pl.ds(8 * b + 4 * h, 4)].reshape(cols, depth)
        return lax.dot_general(lhs[...], block, (((1,), (1,)), ((), ())), preferred_element_type=F32)

    def far_block(e, carry):
        far_out[e] = product((n + 2) % 4, e).astype(BF16)
        far_copy(e).start()
        return carry

    def near_block(e):
        def step(k, carry):
            h = jnp.where(k == 0, 1 - e, e)
            part[h] = product((n + 1 + 2 * e) % 4, h)

            @pl.when(k == 0)
            def _():
                near_out[e, h] = part[h].astype(BF16)
                early_copy(e).start()

            return carry

        lax.fori_loop(0, 2, step, 0)

    def send_late(e):
        far_copy(e).wait_recv()
        near_out[e, e] = (part[e] + far_in[e].astype(F32)).astype(BF16)
        late_copy(e).start()

    lax.fori_loop(0, 2, far_block, 0)
    far_plane.first_near()
    near_block(e1)
    far_plane.second_near(0)
    far_plane.first_far()
    far_plane.second_near(1)
    far_plane.second_far(0)
    far_plane.second_near(2)
    far_plane.second_far(1)
    far_plane.second_near(3)
    send_late(e1)
    far_plane.second_far(2)
    far_plane.second_far(3)
    far_plane.whole().wait_recv()
    near_block(e2)
    send_late(e2)

    def own_block(h, carry):
        span = pl.ds(pl.multiple_of(cols * h, cols), cols)
        part[h] = product(n, h) + x_ref[:, span].astype(F32)
        return carry

    lax.fori_loop(0, 2, own_block, 0)

    def ag(block, h, e, slot):
        return copy(m.at[block, h], m.at[block, h], NARROW_AG + slot, by(e))

    def own_copy(h, e):
        return ag(n, h, e, 2 * e + h)

    def pass_on(e):
        return ag((n + 3 + 2 * e) % 4, e, e, 4 + e)

    early_copy(e2).wait_recv()
    late_copy(e2).wait_recv()

    def finish(k, carry):
        h = jnp.where(k == 0, 1 - e1, e1)

        @pl.when(k == 0)
        def _():
            early_copy(e1).wait_recv()

        @pl.when(k == 1)
        def _():
            late_copy(e1).wait_recv()

        m[n, h] = (part[h] + near_in[0, h].astype(F32) + near_in[1, h].astype(F32)).astype(BF16)
        own_copy(h, 0).start()
        own_copy(h, 1).start()
        return carry

    lax.fori_loop(0, 2, finish, 0)
    igacc[...] = jnp.zeros((tokens, ks), F32)

    def core_copy(d):
        return copy(core_out.at[d], core_in.at[d], CORE_SUM + d, sibling)

    me = 4 * y + x

    def wide_send(d):
        def one(k, carry):
            yy, xx = peer(k)
            copy(
                wide_out.at[d, 4 * yy + xx], wide_in.at[d, me], WIDE_RS + d, {"wide": at(zl, yy, xx)}
            ).start()
            return carry

        lax.fori_loop(1, 16, one, 0)

    def wide_all(d):
        return copy(
            wide_out.at[d, pl.ds(0, 15)], wide_in.at[d, pl.ds(0, 15)], WIDE_RS + d, {"wide": at(zl, y, (x + 1) % 4)}
        )

    def final_copy(d):
        return pltpu.make_async_remote_copy(
            src_ref=fin_out.at[d], dst_ref=fin_in.at[zl, c], send_sem=send_sem.at[FINAL + d],
            recv_sem=recv_sem.at[FINAL + 2 * zl + c], device_id=target(d), device_id_type=MESH,
        )

    def reduce(d):
        wide_all(d).wait_recv()
        total = wide_in[d, 0].astype(F32)
        for k in range(1, 16):
            total = total + wide_in[d, k].astype(F32)
        stays = jnp.logical_and(at_home, d == 0)

        @pl.when(stays)
        def _():
            fin_in[zl, c] = total.astype(BF16)

        @pl.when(jnp.logical_not(stays))
        def _():
            fin_out[d] = total.astype(BF16)
            final_copy(d).start()

    def order(r):
        return jnp.where(r == 0, 0, jnp.where(r == 1, 3, jnp.where(r == 2, 1, 2)))

    def backward(i, carry):
        r = i // 2

        @pl.when(i == 2)
        def _():
            own_copy(0, 0).wait_recv()
            pass_on(0).start()
            own_copy(1, 1).wait_recv()
            pass_on(1).start()
            own_copy(1, 0).wait_recv()

        @pl.when(i == 4)
        def _():
            own_copy(0, 1).wait_recv()

        @pl.when(i == 6)
        def _():
            reduce(0)
            pass_on(0).wait_recv()
            pass_on(1).wait_recv()

        d = order(r)
        h = jnp.where(i % 2 == 0, 1 - c, c)
        b = (n + d) % 4
        piece = m[b, h]
        block = ct[pl.ds(8 * b + 4 * h, 4), :, pl.ds(kt, ks)].reshape(cols, ks)
        grad = jnp.dot(xt_ref[...], piece, preferred_element_type=F32)

        @pl.when(i % 2 == 0)
        def _():
            core_out[d] = grad.astype(BF16)
            core_copy(d).start()

        @pl.when(i % 2 == 1)
        def _():
            kept[...] = grad

        igacc[...] += jnp.dot(piece, block, preferred_element_type=F32)

        @pl.when(i % 2 == 1)
        def _():
            core_copy(d).wait_recv()
            both = (kept[...] + core_in[d].astype(F32)).astype(BF16).reshape(16, half, cols)
            wide_out[d] = both
            wide_in[d, me] = wide_out[d, me]
            wide_send(d)

        return carry

    lax.fori_loop(0, 8, backward, 0)
    for h in range(2):
        span = slice(cols * h, cols * h + cols)
        ig_ref[:, span] = (m[n, h].astype(F32) + igacc[:, span]).astype(BF16)

    def reduce_rest(r, carry):
        reduce(order(r))
        return carry

    lax.fori_loop(1, 4, reduce_rest, 0)
    scale = 1.0 / (tokens * 64.0) ** 0.5
    for zz in range(2):
        for cc in range(2):

            @pl.when(jnp.logical_not(sources[2 * zz + cc][1]))
            def _():
                pltpu.make_async_remote_copy(
                    src_ref=fin_out.at[0], dst_ref=fin_in.at[zz, cc], send_sem=send_sem.at[FINAL],
                    recv_sem=recv_sem.at[FINAL + 2 * zz + cc], device_id=sibling, device_id_type=MESH,
                ).wait_recv()

    for h in range(2):
        wg_ref[:, cols * h : cols * h + cols] = (fin_in[0, h].astype(F32) + fin_in[1, h].astype(F32)) * scale

    for item in sent + sq_copies:
        item.wait_send()
    near_plane.whole().wait_send()
    far_plane.whole().wait_send()
    for e in range(2):
        far_copy(e).wait_send()
        early_copy(e).wait_send()
        late_copy(e).wait_send()
        pass_on(e).wait_send()
        for h in range(2):
            own_copy(h, e).wait_send()
    for d in range(4):
        core_copy(d).wait_send()
        wide_all(d).wait_send()

        @pl.when(jnp.logical_not(jnp.logical_and(at_home, d == 0)))
        def _():
            final_copy(d).wait_send()

    @pl.when(n == owner)
    def _():
        for item in w_copies:
            item.wait_send()


def shards(teacher_rows, teacher_gain, projector, student_rows, student_weight):
    tokens, kt = teacher_rows.shape
    ks = student_rows.shape[1]
    width = projector.shape[1]
    half, cols, depth = width // 2, ks // 2, kt + ks
    c, w = lax.axis_index("section"), lax.axis_index("wide")
    weight_cols = lax.dynamic_slice(student_weight, (0, width * (w % 8) + half * c), (4 * ks, half))
    weight_t = weight_cols.reshape(4, ks, half).transpose(0, 2, 1)
    vmem = pl.BlockSpec(memory_space=pltpu.VMEM)
    return pl.pallas_call(
        kernel,
        out_shape=(
            jax.ShapeDtypeStruct((tokens, ks), BF16),
            jax.ShapeDtypeStruct((half, ks), F32),
        ),
        in_specs=[vmem] * 6,
        out_specs=(vmem, vmem),
        scratch_shapes=[
            pltpu.VMEM((32, width, depth), BF16),
            pltpu.VMEM((tokens, depth), BF16),
            pltpu.VMEM((tokens, kt), BF16),
            pltpu.VMEM((4, 8, 128), F32),
            pltpu.VMEM((2, tokens, cols), F32),
            pltpu.VMEM((2, tokens, cols), BF16),
            pltpu.VMEM((2, 2, tokens, cols), BF16),
            pltpu.VMEM((2, tokens, cols), BF16),
            pltpu.VMEM((2, 2, tokens, cols), BF16),
            pltpu.VMEM((4, 2, tokens, cols), BF16),
            pltpu.VMEM((tokens, ks), F32),
            pltpu.VMEM((ks, cols), F32),
            pltpu.VMEM((4, ks, cols), BF16),
            pltpu.VMEM((4, ks, cols), BF16),
            pltpu.VMEM((4, 16, half, cols), BF16),
            pltpu.VMEM((4, 16, half, cols), BF16),
            pltpu.VMEM((4, half, cols), BF16),
            pltpu.VMEM((2, 2, half, cols), BF16),
            pltpu.SemaphoreType.DMA((SLOTS,)),
            pltpu.SemaphoreType.DMA((SLOTS,)),
        ],
        compiler_params=pltpu.CompilerParams(
            collective_id=0, has_side_effects=True, vmem_limit_bytes=60 * 2**20
        ),
    )(
        teacher_rows,
        teacher_gain.reshape(1, kt),
        projector.T,
        weight_t,
        student_rows,
        student_rows.T,
    )


def solution(mesh):
    placed = (
        P(("section", "wide"), "narrow"),
        P("narrow"),
        P("narrow", "wide"),
        P(("section", "wide"), "narrow"),
        P(None, "narrow"),
    )
    return jax.shard_map(
        shards,
        mesh=mesh,
        in_specs=placed,
        out_specs=(P(("section", "wide"), "narrow"), P(("section", "wide"), "narrow")),
        check_vma=False,
    )
```

```python
import functools

import jax
import jax.numpy as jnp
from jax import lax
from jax.experimental import pallas as pl
from jax.experimental.pallas import tpu as pltpu
from jax.sharding import PartitionSpec as P

MESH = pl.DeviceIdType.MESH
F32 = jnp.float32
BF16 = jnp.bfloat16

GATHER = 0
ZSWAP = 40
WEIGHT = 41
SQUARES = 49
PAIRED = 52
SIBLING = 53
NARROW_RS = 55
NARROW_AG = 61
CORE_SUM = 67
WIDE_RS = 71
FINAL = 75
SLOTS = 79


def kernel(
    t_ref, g_ref, pt_ref, x_ref, weight_ref, ig_ref, wg_ref, window, wt_ref, xt_ref,
    ct, lhs, hid, sq, part, far_out, near_out, far_in, near_in, m, igacc,
    kept, core_out, core_in, wide_out, wide_in, fin_out, fin_in, send_sem, recv_sem, local_sem,
):
    c = lax.axis_index("section")
    w = lax.axis_index("wide")
    n = lax.axis_index("narrow")
    x, y, zl = w % 4, (w // 4) % 4, w // 16
    tokens, kt = t_ref.shape
    ks = x_ref.shape[1]
    half = pt_ref.shape[0] // 2
    depth = kt + ks
    cut = (depth // 256 + 1) * 128
    cols = ks // 2
    rows = pl.ds(pl.multiple_of(half * c, half), half)

    def at(zz, yy, xx):
        return zz * 16 + yy * 4 + xx

    sibling = {"section": 1 - c}
    z_other = {"wide": at(1 - zl, y, x)}
    n_dev = [None] + [{"narrow": (n + d) % 4} for d in (1, 2, 3)]

    def peer(k):
        return (y + k // 4) % 4, (x + k % 4) % 4

    def target(d):
        return {"section": n // 2, "wide": at(n % 2, y, x), "narrow": (n + d) % 4}

    at_home = n == 2 * c + zl
    sources = [
        ({"section": cc, "wide": at(zz, y, x), "narrow": 2 * c + zl}, jnp.logical_and(at_home, jnp.logical_and(cc == c, zz == zl)))
        for zz in range(2)
        for cc in range(2)
    ]

    owner = w // 8
    column = 2 * half * (w % 8) + half * c
    low = jnp.minimum(column // 128 * 128, ks - 256)
    fetch = pltpu.make_async_copy(weight_ref.at[:, pl.ds(pl.multiple_of(low, 128), 256)], window, local_sem)

    @pl.when(n == owner)
    def _():
        fetch.start()

    barrier = pltpu.get_barrier_semaphore()
    z_dev = [{"wide": at(1 - zl, y, x), "narrow": (n + d) % 4} for d in range(4)]
    greeted = [sibling, n_dev[1], n_dev[2], n_dev[3]] + z_dev
    for device in greeted:
        pl.semaphore_signal(barrier, inc=1, device_id=device, device_id_type=MESH)

    def greet(k, carry):
        yy, xx = peer(k)
        pl.semaphore_signal(barrier, inc=1, device_id={"wide": at(zl, yy, xx)}, device_id_type=MESH)
        return carry

    lax.fori_loop(1, 16, greet, 0)
    for device, mine in sources:

        @pl.when(jnp.logical_not(mine))
        def _():
            pl.semaphore_signal(barrier, inc=1, device_id=device, device_id_type=MESH)

    pl.semaphore_wait(barrier, jnp.where(at_home, len(greeted) + 18, len(greeted) + 19))

    def copy(src, dst, slot, device):
        return pltpu.make_async_remote_copy(
            src_ref=src, dst_ref=dst, send_sem=send_sem.at[slot], recv_sem=recv_sem.at[slot],
            device_id=device, device_id_type=MESH,
        )

    w_cols, p_cols = pl.ds(kt, ks), pl.ds(0, kt)

    def weight_copy(k):
        return pltpu.make_async_remote_copy(
            src_ref=wt_ref.at[(n + k) % 4], dst_ref=ct.at[w, rows, w_cols], send_sem=send_sem.at[WEIGHT + k],
            recv_sem=recv_sem.at[WEIGHT + k // 4], device_id=(n_dev[k] if k < 4 else z_dev[k - 4]),
            device_id_type=MESH,
        )

    w_other = at(1 - zl, y, x)
    ct[w, rows, p_cols] = pt_ref[rows, :]
    z_copy = copy(ct.at[w, rows, p_cols], ct.at[w, rows, p_cols], ZSWAP, z_other)
    z_copy.start()

    @pl.when(n == owner)
    def _():
        fetch.wait()
        row = lax.broadcasted_iota(jnp.int32, (half, 256), 0)
        lane = lax.broadcasted_iota(jnp.int32, (half, 256), 1)
        pick = jnp.where(lane == row + (column - low), 1.0, 0.0).astype(BF16)
        for q in range(4):
            wt_ref[q] = lax.dot_general(
                pick, window[ks * q : ks * q + ks, :], (((1,), (1,)), ((), ())), preferred_element_type=F32
            ).astype(BF16)
        for k in (1, 5, 2, 6, 3, 7, 4):
            weight_copy(k).start()
        ct[w, rows, w_cols] = wt_ref[n]

    eye = lax.broadcasted_iota(jnp.int32, (128, 128), 0) == lax.broadcasted_iota(jnp.int32, (128, 128), 1)
    groups = tokens // 128
    sq[0] = jnp.zeros((8, 128), F32)
    for i in range(groups):
        part_t = t_ref[128 * i : 128 * i + 128, :].astype(F32)
        col = jnp.sum(part_t * part_t, axis=1, keepdims=True)
        sq[0, i : i + 1, :] = jnp.sum(jnp.where(eye, col, 0.0), axis=0, keepdims=True)
    sq_copies = [copy(sq.at[0], sq.at[d], SQUARES + d - 1, n_dev[d]) for d in (1, 2, 3)]
    for item in sq_copies:
        item.start()

    def weight_arrives(plane):
        @pl.when(jnp.logical_and(zl == plane, n != owner))
        def _():
            weight_copy(1).wait_recv()

        @pl.when(zl != plane)
        def _():
            weight_copy(5).wait_recv()
            z_copy.wait_recv()

    def slab(index, part=None):
        if part is None:
            return ct.at[index, rows]
        return ct.at[index, rows, pl.ds(0, cut) if part == 0 else pl.ds(cut, depth - cut)]

    def spread(index, slot, device, part=None):
        return copy(slab(index, part), slab(index, part), slot, device)

    sent = []

    def go(item):
        item.start()
        sent.append(item)

    along_a, along_b = jnp.where(c == 0, x, y), jnp.where(c == 0, y, x)

    def cell(plane, da, db):
        a, b = (along_a + da) % 4, (along_b + db) % 4
        return plane * 16 + jnp.where(c == 0, 4 * b + a, 4 * a + b)

    first = [{"wide": cell(zl, 1, 0)}, {"wide": cell(zl, 3, 0)}, {"wide": cell(zl, 2, 0)}]
    second = [{"wide": cell(zl, 0, 1)}, {"wide": cell(zl, 0, 3)}]
    ALONG = (0, 3, 1, 2)

    class Plane:
        def __init__(self, p, plane):
            self.base, self.p, self.plane = GATHER + 20 * p, p, plane

        def to_sibling(self, index):
            copy(slab(index), slab(index), SIBLING + self.p, sibling).start()

        def whole(self):
            planes = ct.at[pl.ds(16 * self.plane, 16), rows]
            return copy(planes, planes, SIBLING + self.p, sibling)

        def begin(self):
            weight_arrives(self.plane)
            own = cell(self.plane, 0, 0)
            for side in range(3):
                go(spread(own, self.base + side, first[side]))
            self.second_send(0)
            self.to_sibling(own)

        def second_send(self, j):
            index = cell(self.plane, ALONG[j], 0)
            for side in range(2):
                go(spread(index, self.base + 4 + 4 * j + side, second[side]))

        def first_near(self):
            for side in range(2):
                index = cell(self.plane, ALONG[1 + side], 0)
                spread(index, self.base + side, first[side]).wait_recv()
                self.second_send(1 + side)
                self.to_sibling(index)

        def first_far(self):
            index = cell(self.plane, 2, 0)
            spread(index, self.base + 2, first[2]).wait_recv()
            self.second_send(3)
            self.to_sibling(index)

        def second_near(self, j):
            slot = self.base + 4 + 4 * j
            for side in range(2):
                index = cell(self.plane, ALONG[j], 3 if side == 0 else 1)
                spread(index, slot + side, second[side]).wait_recv()
                go(spread(index, slot + 2 + side, second[side], side))
                self.to_sibling(index)

        def second_far(self, j):
            slot = self.base + 4 + 4 * j
            index = cell(self.plane, ALONG[j], 2)
            for side in range(2):
                spread(index, slot + 2 + side, second[side], side).wait_recv()
            self.to_sibling(index)

    p_first = 1 - n // 2
    near_plane, far_plane = Plane(0, p_first), Plane(1, 1 - p_first)
    near_plane.begin()

    lhs[:, kt:] = x_ref[...]
    xt_ref[...] = x_ref[...].T
    for item in sq_copies:
        item.wait_recv()
    inverse = lax.rsqrt((sq[0] + sq[1] + sq[2] + sq[3]) / (4 * kt) + 1e-05)
    gain = g_ref[...].astype(F32).reshape(1, kt)
    for i in range(groups):
        col = jnp.sum(jnp.where(eye, inverse[i : i + 1, :], 0.0), axis=1, keepdims=True)
        span = slice(128 * i, 128 * i + 128)
        hid[span, :] = -(t_ref[span, :].astype(F32) * col * gain).astype(BF16)
    paired_copy = copy(hid, lhs.at[:, pl.ds(0, kt)], PAIRED, sibling)
    go(paired_copy)

    near_plane.first_near()
    near_plane.second_near(0)
    near_plane.first_far()
    near_plane.second_near(1)
    near_plane.second_far(0)
    near_plane.second_near(2)
    near_plane.second_far(1)
    far_plane.begin()
    near_plane.second_near(3)
    near_plane.second_far(2)
    near_plane.second_far(3)
    paired_copy.wait_recv()
    near_plane.whole().wait_recv()

    e2 = n % 2
    e1 = 1 - e2

    def by(e):
        return {"narrow": (n + 1 + 2 * e) % 4}

    def far_copy(e):
        return copy(far_out.at[e], far_in.at[e], NARROW_RS + e, by(e))

    def early_copy(e):
        return copy(near_out.at[e, 1 - e], near_in.at[e, 1 - e], NARROW_RS + 2 + e, by(e))

    def late_copy(e):
        return copy(near_out.at[e, e], near_in.at[e, e], NARROW_RS + 4 + e, by(e))

    def product(b, h):
        block = ct[pl.ds(8 * b + 4 * h, 4)].reshape(cols, depth)
        return lax.dot_general(lhs[...], block, (((1,), (1,)), ((), ())), preferred_element_type=F32)

    def far_block(e, carry):
        far_out[e] = product((n + 2) % 4, e).astype(BF16)
        far_copy(e).start()
        return carry

    def near_block(e):
        def step(k, carry):
            h = jnp.where(k == 0, 1 - e, e)
            part[h] = product((n + 1 + 2 * e) % 4, h)

            @pl.when(k == 0)
            def _():
                near_out[e, h] = part[h].astype(BF16)
                early_copy(e).start()

            return carry

        lax.fori_loop(0, 2, step, 0)

    def send_late(e):
        far_copy(e).wait_recv()
        near_out[e, e] = (part[e] + far_in[e].astype(F32)).astype(BF16)
        late_copy(e).start()

    lax.fori_loop(0, 2, far_block, 0)
    far_plane.first_near()
    near_block(e1)
    far_plane.second_near(0)
    far_plane.first_far()
    far_plane.second_near(1)
    far_plane.second_far(0)
    far_plane.second_near(2)
    far_plane.second_far(1)
    far_plane.second_near(3)
    send_late(e1)
    far_plane.second_far(2)
    far_plane.second_far(3)
    far_plane.whole().wait_recv()
    near_block(e2)
    send_late(e2)

    def own_block(h, carry):
        span = pl.ds(pl.multiple_of(cols * h, cols), cols)
        part[h] = product(n, h) + x_ref[:, span].astype(F32)
        return carry

    lax.fori_loop(0, 2, own_block, 0)

    def ag(block, h, e, slot):
        return copy(m.at[block, h], m.at[block, h], NARROW_AG + slot, by(e))

    def own_copy(h, e):
        return ag(n, h, e, 2 * e + h)

    def pass_on(e):
        return ag((n + 3 + 2 * e) % 4, e, e, 4 + e)

    early_copy(e2).wait_recv()
    late_copy(e2).wait_recv()

    def finish(k, carry):
        h = jnp.where(k == 0, 1 - e1, e1)

        @pl.when(k == 0)
        def _():
            early_copy(e1).wait_recv()

        @pl.when(k == 1)
        def _():
            late_copy(e1).wait_recv()

        m[n, h] = (part[h] + near_in[0, h].astype(F32) + near_in[1, h].astype(F32)).astype(BF16)
        own_copy(h, 0).start()
        own_copy(h, 1).start()
        return carry

    lax.fori_loop(0, 2, finish, 0)
    igacc[...] = jnp.zeros((tokens, ks), F32)

    def core_copy(d):
        return copy(core_out.at[d], core_in.at[d], CORE_SUM + d, sibling)

    me = 4 * y + x

    def wide_send(d):
        def one(k, carry):
            yy, xx = peer(k)
            copy(
                wide_out.at[d, 4 * yy + xx], wide_in.at[d, me], WIDE_RS + d, {"wide": at(zl, yy, xx)}
            ).start()
            return carry

        lax.fori_loop(1, 16, one, 0)

    def wide_all(d):
        return copy(
            wide_out.at[d, pl.ds(0, 15)], wide_in.at[d, pl.ds(0, 15)], WIDE_RS + d, {"wide": at(zl, y, (x + 1) % 4)}
        )

    def final_copy(d):
        return pltpu.make_async_remote_copy(
            src_ref=fin_out.at[d], dst_ref=fin_in.at[zl, c], send_sem=send_sem.at[FINAL + d],
            recv_sem=recv_sem.at[FINAL + 2 * zl + c], device_id=target(d), device_id_type=MESH,
        )

    def reduce(d):
        wide_all(d).wait_recv()
        total = wide_in[d, 0].astype(F32)
        for k in range(1, 16):
            total = total + wide_in[d, k].astype(F32)
        stays = jnp.logical_and(at_home, d == 0)

        @pl.when(stays)
        def _():
            fin_in[zl, c] = total.astype(BF16)

        @pl.when(jnp.logical_not(stays))
        def _():
            fin_out[d] = total.astype(BF16)
            final_copy(d).start()

    def order(r):
        return jnp.where(r == 0, 0, jnp.where(r == 1, 3, jnp.where(r == 2, 1, 2)))

    def backward(i, carry):
        r = i // 2

        @pl.when(i == 2)
        def _():
            own_copy(0, 0).wait_recv()
            pass_on(0).start()
            own_copy(1, 1).wait_recv()
            pass_on(1).start()
            own_copy(1, 0).wait_recv()

        @pl.when(i == 4)
        def _():
            own_copy(0, 1).wait_recv()

        @pl.when(i == 6)
        def _():
            reduce(0)
            pass_on(0).wait_recv()
            pass_on(1).wait_recv()

        d = order(r)
        h = jnp.where(i % 2 == 0, 1 - c, c)
        b = (n + d) % 4
        piece = m[b, h]
        block = ct[pl.ds(8 * b + 4 * h, 4), :, pl.ds(kt, ks)].reshape(cols, ks)
        grad = jnp.dot(xt_ref[...], piece, preferred_element_type=F32)

        @pl.when(i % 2 == 0)
        def _():
            core_out[d] = grad.astype(BF16)
            core_copy(d).start()

        @pl.when(i % 2 == 1)
        def _():
            kept[...] = grad

        igacc[...] += jnp.dot(piece, block, preferred_element_type=F32)

        @pl.when(i % 2 == 1)
        def _():
            core_copy(d).wait_recv()
            both = (kept[...] + core_in[d].astype(F32)).astype(BF16).reshape(16, half, cols)
            wide_out[d] = both
            wide_in[d, me] = wide_out[d, me]
            wide_send(d)

        return carry

    lax.fori_loop(0, 8, backward, 0)
    for h in range(2):
        span = slice(cols * h, cols * h + cols)
        ig_ref[:, span] = (m[n, h].astype(F32) + igacc[:, span]).astype(BF16)

    def reduce_rest(r, carry):
        reduce(order(r))
        return carry

    lax.fori_loop(1, 4, reduce_rest, 0)
    scale = 1.0 / (tokens * 64.0) ** 0.5
    for zz in range(2):
        for cc in range(2):

            @pl.when(jnp.logical_not(sources[2 * zz + cc][1]))
            def _():
                pltpu.make_async_remote_copy(
                    src_ref=fin_out.at[0], dst_ref=fin_in.at[zz, cc], send_sem=send_sem.at[FINAL],
                    recv_sem=recv_sem.at[FINAL + 2 * zz + cc], device_id=sibling, device_id_type=MESH,
                ).wait_recv()

    for h in range(2):
        wg_ref[:, cols * h : cols * h + cols] = (fin_in[0, h].astype(F32) + fin_in[1, h].astype(F32)) * scale

    for item in sent + sq_copies + [z_copy]:
        item.wait_send()
    near_plane.whole().wait_send()
    far_plane.whole().wait_send()
    for e in range(2):
        far_copy(e).wait_send()
        early_copy(e).wait_send()
        late_copy(e).wait_send()
        pass_on(e).wait_send()
        for h in range(2):
            own_copy(h, e).wait_send()
    for d in range(4):
        core_copy(d).wait_send()
        wide_all(d).wait_send()

        @pl.when(jnp.logical_not(jnp.logical_and(at_home, d == 0)))
        def _():
            final_copy(d).wait_send()

    @pl.when(n == owner)
    def _():
        for k in range(1, 8):
            weight_copy(k).wait_send()


def shards(teacher_rows, teacher_gain, projector, student_rows, student_weight):
    tokens, kt = teacher_rows.shape
    ks = student_rows.shape[1]
    width = projector.shape[1]
    half, cols, depth = width // 2, ks // 2, kt + ks
    vmem = pl.BlockSpec(memory_space=pltpu.VMEM)
    return pl.pallas_call(
        kernel,
        out_shape=(
            jax.ShapeDtypeStruct((tokens, ks), BF16),
            jax.ShapeDtypeStruct((half, ks), F32),
        ),
        in_specs=[vmem] * 4 + [pl.BlockSpec(memory_space=pl.ANY)],
        out_specs=(vmem, vmem),
        scratch_shapes=[
            pltpu.VMEM((4 * ks, 256), BF16),
            pltpu.VMEM((4, half, ks), BF16),
            pltpu.VMEM((ks, tokens), BF16),
            pltpu.VMEM((32, width, depth), BF16),
            pltpu.VMEM((tokens, depth), BF16),
            pltpu.VMEM((tokens, kt), BF16),
            pltpu.VMEM((4, 8, 128), F32),
            pltpu.VMEM((2, tokens, cols), F32),
            pltpu.VMEM((2, tokens, cols), BF16),
            pltpu.VMEM((2, 2, tokens, cols), BF16),
            pltpu.VMEM((2, tokens, cols), BF16),
            pltpu.VMEM((2, 2, tokens, cols), BF16),
            pltpu.VMEM((4, 2, tokens, cols), BF16),
            pltpu.VMEM((tokens, ks), F32),
            pltpu.VMEM((ks, cols), F32),
            pltpu.VMEM((4, ks, cols), BF16),
            pltpu.VMEM((4, ks, cols), BF16),
            pltpu.VMEM((4, 16, half, cols), BF16),
            pltpu.VMEM((4, 16, half, cols), BF16),
            pltpu.VMEM((4, half, cols), BF16),
            pltpu.VMEM((2, 2, half, cols), BF16),
            pltpu.SemaphoreType.DMA((SLOTS,)),
            pltpu.SemaphoreType.DMA((SLOTS,)),
            pltpu.SemaphoreType.DMA,
        ],
        compiler_params=pltpu.CompilerParams(
            collective_id=0, has_side_effects=True, vmem_limit_bytes=60 * 2**20
        ),
    )(
        teacher_rows,
        teacher_gain,
        projector.T,
        student_rows,
        student_weight,
    )


def solution(mesh):
    placed = (
        P(("section", "wide"), "narrow"),
        P("narrow"),
        P("narrow", "wide"),
        P(("section", "wide"), "narrow"),
        P(None, "narrow"),
    )
    return jax.shard_map(
        shards,
        mesh=mesh,
        in_specs=placed,
        out_specs=(P(("section", "wide"), "narrow"), P(("section", "wide"), "narrow")),
        check_vma=False,
    )
```

```python
import functools

import jax
import jax.numpy as jnp
from jax import lax
from jax.experimental import pallas as pl
from jax.experimental.pallas import tpu as pltpu
from jax.sharding import PartitionSpec as P

MESH = pl.DeviceIdType.MESH
F32 = jnp.float32
BF16 = jnp.bfloat16

GATHER = 0
ZSWAP = 40
WEIGHT = 41
SQUARES = 45
PAIRED = 48
SIBLING = 49
NARROW_RS = 51
NARROW_AG = 57
CORE_SUM = 65
WIDE_RS = 70
FINAL = 75
SLOTS = 79


def kernel(
    t_ref, g_ref, pt_ref, x_ref, weight_ref, ig_ref, wg_ref, window, wt_ref, xt_ref,
    ct, lhs, hid, sq, part, far_out, near_out, far_in, near_in, m, igacc,
    kept, core_out, core_in, wide_out, wide_in, fin_out, fin_in, send_sem, recv_sem, local_sem,
):
    c = lax.axis_index("section")
    w = lax.axis_index("wide")
    n = lax.axis_index("narrow")
    x, y, zl = w % 4, (w // 4) % 4, w // 16
    tokens, kt = t_ref.shape
    ks = x_ref.shape[1]
    half = pt_ref.shape[0] // 2
    depth = kt + ks
    cut = (depth // 256 + 1) * 128
    cols = ks // 2
    rows = pl.ds(pl.multiple_of(half * c, half), half)

    def at(zz, yy, xx):
        return zz * 16 + yy * 4 + xx

    sibling = {"section": 1 - c}
    z_other = {"wide": at(1 - zl, y, x)}
    n_dev = [None] + [{"narrow": (n + d) % 4} for d in (1, 2, 3)]

    def peer(k):
        return (y + k // 4) % 4, (x + k % 4) % 4

    def target(d):
        return {"section": n // 2, "wide": at(n % 2, y, x), "narrow": (n + d) % 4}

    at_home = n == 2 * c + zl
    sources = [
        ({"section": cc, "wide": at(zz, y, x), "narrow": 2 * c + zl}, jnp.logical_and(at_home, jnp.logical_and(cc == c, zz == zl)))
        for zz in range(2)
        for cc in range(2)
    ]

    holder = n % 2 == y // 2
    w_slab = at(n // 2, y, x)
    column = 2 * half * (w % 8) + half * c
    low = jnp.minimum(column // 128 * 128, ks - 256)
    fetch = pltpu.make_async_copy(weight_ref.at[:, pl.ds(pl.multiple_of(low, 128), 256)], window, local_sem)

    @pl.when(holder)
    def _():
        fetch.start()

    barrier = pltpu.get_barrier_semaphore()
    greeted = [sibling, z_other, n_dev[1], n_dev[2], n_dev[3]]
    for device in greeted:
        pl.semaphore_signal(barrier, inc=1, device_id=device, device_id_type=MESH)

    def greet(k, carry):
        yy, xx = peer(k)
        pl.semaphore_signal(barrier, inc=1, device_id={"wide": at(zl, yy, xx)}, device_id_type=MESH)
        return carry

    lax.fori_loop(1, 16, greet, 0)
    for device, mine in sources:

        @pl.when(jnp.logical_not(mine))
        def _():
            pl.semaphore_signal(barrier, inc=1, device_id=device, device_id_type=MESH)

    pl.semaphore_wait(barrier, jnp.where(at_home, len(greeted) + 18, len(greeted) + 19))

    def copy(src, dst, slot, device):
        return pltpu.make_async_remote_copy(
            src_ref=src, dst_ref=dst, send_sem=send_sem.at[slot], recv_sem=recv_sem.at[slot],
            device_id=device, device_id_type=MESH,
        )

    w_cols, p_cols = pl.ds(kt, ks), pl.ds(0, kt)

    def weight_copy(k, plane):
        return pltpu.make_async_remote_copy(
            src_ref=wt_ref.at[(n + k) % 4], dst_ref=ct.at[w_slab, rows, w_cols], send_sem=send_sem.at[WEIGHT + k],
            recv_sem=recv_sem.at[WEIGHT + plane], device_id=n_dev[k], device_id_type=MESH,
        )

    ct[w, rows, p_cols] = pt_ref[rows, :]
    z_copy = copy(ct.at[w, rows, p_cols], ct.at[w, rows, p_cols], ZSWAP, z_other)
    z_copy.start()

    @pl.when(holder)
    def _():
        fetch.wait()
        row = lax.broadcasted_iota(jnp.int32, (half, 256), 0)
        lane = lax.broadcasted_iota(jnp.int32, (half, 256), 1)
        pick = jnp.where(lane == row + (column - low), 1.0, 0.0).astype(BF16)
        for q in range(4):
            wt_ref[q] = lax.dot_general(
                pick, window[ks * q : ks * q + ks, :], (((1,), (1,)), ((), ())), preferred_element_type=F32
            ).astype(BF16)
        for k in (2, 1, 3):
            weight_copy(k, n // 2).start()
        ct[w_slab, rows, w_cols] = wt_ref[n]

    def weight_arrives(plane):
        @pl.when(n != 2 * plane + y // 2)
        def _():
            weight_copy(1, plane).wait_recv()

        @pl.when(zl != plane)
        def _():
            z_copy.wait_recv()

    def slab(index, part=None):
        if part is None:
            return ct.at[index, rows]
        return ct.at[index, rows, pl.ds(0, cut) if part == 0 else pl.ds(cut, depth - cut)]

    def spread(index, slot, device, part=None):
        return copy(slab(index, part), slab(index, part), slot, device)

    sent = []

    def go(item):
        item.start()
        sent.append(item)

    along_a, along_b = jnp.where(c == 0, x, y), jnp.where(c == 0, y, x)

    def cell(plane, da, db):
        a, b = (along_a + da) % 4, (along_b + db) % 4
        return plane * 16 + jnp.where(c == 0, 4 * b + a, 4 * a + b)

    first = [{"wide": cell(zl, 1, 0)}, {"wide": cell(zl, 3, 0)}, {"wide": cell(zl, 2, 0)}]
    second = [{"wide": cell(zl, 0, 1)}, {"wide": cell(zl, 0, 3)}]
    ALONG = (0, 3, 1, 2)

    class Plane:
        def __init__(self, p, plane):
            self.base, self.p, self.plane = GATHER + 20 * p, p, plane

        def to_sibling(self, index):
            copy(slab(index), slab(index), SIBLING + self.p, sibling).start()

        def whole(self):
            planes = ct.at[pl.ds(16 * self.plane, 16), rows]
            return copy(planes, planes, SIBLING + self.p, sibling)

        def begin(self):
            weight_arrives(self.plane)
            own = cell(self.plane, 0, 0)
            for side in range(3):
                go(spread(own, self.base + side, first[side]))
            self.second_send(0)
            self.to_sibling(own)

        def second_send(self, j):
            index = cell(self.plane, ALONG[j], 0)
            for side in range(2):
                go(spread(index, self.base + 4 + 4 * j + side, second[side]))

        def first_near(self):
            for side in range(2):
                index = cell(self.plane, ALONG[1 + side], 0)
                spread(index, self.base + side, first[side]).wait_recv()
                self.second_send(1 + side)
                self.to_sibling(index)

        def first_far(self):
            index = cell(self.plane, 2, 0)
            spread(index, self.base + 2, first[2]).wait_recv()
            self.second_send(3)
            self.to_sibling(index)

        def second_near(self, j):
            slot = self.base + 4 + 4 * j
            for side in range(2):
                index = cell(self.plane, ALONG[j], 3 if side == 0 else 1)
                spread(index, slot + side, second[side]).wait_recv()
                go(spread(index, slot + 2 + side, second[side], side))
                self.to_sibling(index)

        def second_far(self, j):
            slot = self.base + 4 + 4 * j
            index = cell(self.plane, ALONG[j], 2)
            for side in range(2):
                spread(index, slot + 2 + side, second[side], side).wait_recv()
            self.to_sibling(index)

    p_first = 1 - n // 2
    near_plane, far_plane = Plane(0, p_first), Plane(1, 1 - p_first)
    near_plane.begin()

    eye = lax.broadcasted_iota(jnp.int32, (128, 128), 0) == lax.broadcasted_iota(jnp.int32, (128, 128), 1)
    groups = tokens // 128
    sq[0] = jnp.zeros((8, 128), F32)
    for i in range(groups):
        part_t = t_ref[128 * i : 128 * i + 128, :].astype(F32)
        col = jnp.sum(part_t * part_t, axis=1, keepdims=True)
        sq[0, i : i + 1, :] = jnp.sum(jnp.where(eye, col, 0.0), axis=0, keepdims=True)
    sq_copies = [copy(sq.at[0], sq.at[d], SQUARES + d - 1, n_dev[d]) for d in (1, 2, 3)]
    for item in sq_copies:
        item.start()

    lhs[:, kt:] = x_ref[...]
    xt_ref[...] = x_ref[...].T
    for item in sq_copies:
        item.wait_recv()
    inverse = lax.rsqrt((sq[0] + sq[1] + sq[2] + sq[3]) / (4 * kt) + 1e-05)
    gain = g_ref[...].astype(F32).reshape(1, kt)
    for i in range(groups):
        col = jnp.sum(jnp.where(eye, inverse[i : i + 1, :], 0.0), axis=1, keepdims=True)
        span = slice(128 * i, 128 * i + 128)
        hid[span, :] = -(t_ref[span, :].astype(F32) * col * gain).astype(BF16)
    paired_copy = copy(hid, lhs.at[:, pl.ds(0, kt)], PAIRED, sibling)
    go(paired_copy)

    near_plane.first_near()
    near_plane.second_near(0)
    near_plane.first_far()
    near_plane.second_near(1)
    near_plane.second_far(0)
    near_plane.second_near(2)
    near_plane.second_far(1)
    far_plane.begin()
    near_plane.second_near(3)
    near_plane.second_far(2)
    near_plane.second_far(3)
    paired_copy.wait_recv()
    near_plane.whole().wait_recv()

    e2 = n % 2
    e1 = 1 - e2

    def by(e):
        return {"narrow": (n + 1 + 2 * e) % 4}

    def far_copy(e):
        return copy(far_out.at[e], far_in.at[e], NARROW_RS + e, by(e))

    def early_copy(e):
        return copy(near_out.at[e, 1 - e], near_in.at[e, 1 - e], NARROW_RS + 2 + e, by(e))

    def late_copy(e):
        return copy(near_out.at[e, e], near_in.at[e, e], NARROW_RS + 4 + e, by(e))

    def product(b, h):
        block = ct[pl.ds(8 * b + 4 * h, 4)].reshape(cols, depth)
        return lax.dot_general(lhs[...], block, (((1,), (1,)), ((), ())), preferred_element_type=F32)

    def far_block(e, carry):
        far_out[e] = product((n + 2) % 4, e).astype(BF16)
        far_copy(e).start()
        return carry

    def near_block(e):
        def step(k, carry):
            h = jnp.where(k == 0, 1 - e, e)
            part[h] = product((n + 1 + 2 * e) % 4, h)

            @pl.when(k == 0)
            def _():
                near_out[e, h] = part[h].astype(BF16)
                early_copy(e).start()

            return carry

        lax.fori_loop(0, 2, step, 0)

    def send_late(e):
        far_copy(e).wait_recv()
        near_out[e, e] = (part[e] + far_in[e].astype(F32)).astype(BF16)
        late_copy(e).start()

    lax.fori_loop(0, 2, far_block, 0)
    far_plane.first_near()
    near_block(e1)
    far_plane.second_near(0)
    far_plane.first_far()
    far_plane.second_near(1)
    far_plane.second_far(0)
    far_plane.second_near(2)
    far_plane.second_far(1)
    far_plane.second_near(3)
    send_late(e1)
    far_plane.second_far(2)
    far_plane.second_far(3)
    far_plane.whole().wait_recv()
    near_block(e2)
    send_late(e2)

    def own_block(h, carry):
        span = pl.ds(pl.multiple_of(cols * h, cols), cols)
        part[h] = product(n, h) + x_ref[:, span].astype(F32)
        return carry

    lax.fori_loop(0, 2, own_block, 0)

    wide_part = 2 * cols // 3
    PARTS = (pl.ds(0, wide_part), pl.ds(wide_part, cols - wide_part))

    def own_copy(h, e):
        return copy(m.at[n, h], m.at[n, h], NARROW_AG + 2 * e + h, by(e))

    def pass_on(e, s):
        piece = m.at[(n + 3 + 2 * e) % 4, e, :, PARTS[s]]
        return copy(piece, piece, NARROW_AG + 4 + 2 * e + s, by(e))

    early_copy(e2).wait_recv()
    late_copy(e2).wait_recv()

    def finish(k, carry):
        h = jnp.where(k == 0, 1 - e1, e1)

        @pl.when(k == 0)
        def _():
            early_copy(e1).wait_recv()

        @pl.when(k == 1)
        def _():
            late_copy(e1).wait_recv()

        m[n, h] = (part[h] + near_in[0, h].astype(F32) + near_in[1, h].astype(F32)).astype(BF16)
        own_copy(h, 0).start()
        own_copy(h, 1).start()
        return carry

    lax.fori_loop(0, 2, finish, 0)
    igacc[...] = jnp.zeros((tokens, ks), F32)
    me = 4 * y + x

    def core_copy(d, columns, slot):
        return copy(core_out.at[d, :, columns], core_in.at[d, :, columns], CORE_SUM + slot, sibling)

    def wide_send(d, columns, slot):
        def one(k, carry):
            yy, xx = peer(k)
            copy(
                wide_out.at[d, 4 * yy + xx, :, columns], wide_in.at[d, me, :, columns], WIDE_RS + slot,
                {"wide": at(zl, yy, xx)},
            ).start()
            return carry

        lax.fori_loop(1, 16, one, 0)

    def wide_all(d, columns, slot):
        return copy(
            wide_out.at[d, pl.ds(0, 15), :, columns], wide_in.at[d, pl.ds(0, 15), :, columns], WIDE_RS + slot,
            {"wide": at(zl, y, (x + 1) % 4)},
        )

    def gradient(d, columns, slot):
        b = (n + d) % 4
        core_out[d, :, columns] = jnp.dot(
            xt_ref[...], m[b, 1 - c, :, columns], preferred_element_type=F32
        ).astype(BF16)
        core_copy(d, columns, slot).start()
        kept[:, columns] = jnp.dot(xt_ref[...], m[b, c, :, columns], preferred_element_type=F32)

    def chip_sum(d, columns, slot):
        core_copy(d, columns, slot).wait_recv()
        both = (kept[:, columns] + core_in[d, :, columns].astype(F32)).astype(BF16)
        wide_out[d, :, :, columns] = both.reshape(16, half, columns.size)
        wide_in[d, me, :, columns] = wide_out[d, me, :, columns]
        wide_send(d, columns, slot)

    def backward(d):
        b = (n + d) % 4
        for h in range(2):
            block = ct[pl.ds(8 * b + 4 * h, 4), :, pl.ds(kt, ks)].reshape(cols, ks)
            igacc[...] += jnp.dot(m[b, h], block, preferred_element_type=F32)

    def final_copy(d):
        return pltpu.make_async_remote_copy(
            src_ref=fin_out.at[d], dst_ref=fin_in.at[zl, c], send_sem=send_sem.at[FINAL + d],
            recv_sem=recv_sem.at[FINAL + 2 * zl + c], device_id=target(d), device_id_type=MESH,
        )

    def reduce(d):
        total = wide_in[d, 0].astype(F32)
        for k in range(1, 16):
            total = total + wide_in[d, k].astype(F32)
        stays = jnp.logical_and(at_home, d == 0)

        @pl.when(stays)
        def _():
            fin_in[zl, c] = total.astype(BF16)

        @pl.when(jnp.logical_not(stays))
        def _():
            fin_out[d] = total.astype(BF16)
            final_copy(d).start()

    ALL = pl.ds(0, cols)

    def near_gradient(r, carry):
        @pl.when(r == 1)
        def _():
            own_copy(0, 0).wait_recv()
            pass_on(0, 0).start()
            pass_on(0, 1).start()
            own_copy(1, 1).wait_recv()
            pass_on(1, 0).start()
            pass_on(1, 1).start()
            own_copy(1, 0).wait_recv()

        @pl.when(r == 2)
        def _():
            own_copy(0, 1).wait_recv()

        d = jnp.where(r == 0, 0, jnp.where(r == 1, 3, 1))
        slot = jnp.where(d == 3, 2, d)
        gradient(d, ALL, slot)
        backward(d)
        chip_sum(d, ALL, slot)
        return carry

    lax.fori_loop(0, 3, near_gradient, 0)
    wide_all(0, ALL, 0).wait_recv()
    reduce(0)
    for item in sent + sq_copies + [z_copy]:
        item.wait_send()
    near_plane.whole().wait_send()
    far_plane.whole().wait_send()
    for e in range(2):
        far_copy(e).wait_send()
        early_copy(e).wait_send()
        late_copy(e).wait_send()

    @pl.when(holder)
    def _():
        for k in range(1, 4):
            weight_copy(k, n // 2).wait_send()

    for s in range(2):
        for e in range(2):
            pass_on(e, s).wait_recv()
        gradient(2, PARTS[s], 3 + s)
        chip_sum(2, PARTS[s], 3 + s)
    backward(2)
    for h in range(2):
        span = slice(cols * h, cols * h + cols)
        ig_ref[:, span] = (m[n, h].astype(F32) + igacc[:, span]).astype(BF16)
    wide_all(3, ALL, 2).wait_recv()
    reduce(3)
    wide_all(1, ALL, 1).wait_recv()
    reduce(1)
    for s in range(2):
        wide_all(2, PARTS[s], 3 + s).wait_recv()
    reduce(2)

    def late_waits():
        for e in range(2):
            for k in range(2):
                pass_on(e, k).wait_send()
                own_copy(k, e).wait_send()
        for d, columns, slot in ((0, ALL, 0), (1, ALL, 1), (3, ALL, 2), (2, PARTS[0], 3), (2, PARTS[1], 4)):
            core_copy(d, columns, slot).wait_send()
            wide_all(d, columns, slot).wait_send()
        for d in range(4):

            @pl.when(jnp.logical_not(jnp.logical_and(at_home, d == 0)))
            def _():
                final_copy(d).wait_send()

    scale = 1.0 / (tokens * 64.0) ** 0.5
    for zz in range(2):
        for cc in range(2):

            @pl.when(jnp.logical_not(sources[2 * zz + cc][1]))
            def _():
                pltpu.make_async_remote_copy(
                    src_ref=fin_out.at[0], dst_ref=fin_in.at[zz, cc], send_sem=send_sem.at[FINAL],
                    recv_sem=recv_sem.at[FINAL + 2 * zz + cc], device_id=sibling, device_id_type=MESH,
                ).wait_recv()

    for h in range(2):
        wg_ref[:, cols * h : cols * h + cols] = (fin_in[0, h].astype(F32) + fin_in[1, h].astype(F32)) * scale

    late_waits()


def shards(teacher_rows, teacher_gain, projector, student_rows, student_weight):
    tokens, kt = teacher_rows.shape
    ks = student_rows.shape[1]
    width = projector.shape[1]
    half, cols, depth = width // 2, ks // 2, kt + ks
    vmem = pl.BlockSpec(memory_space=pltpu.VMEM)
    return pl.pallas_call(
        kernel,
        out_shape=(
            jax.ShapeDtypeStruct((tokens, ks), BF16),
            jax.ShapeDtypeStruct((half, ks), F32),
        ),
        in_specs=[vmem] * 4 + [pl.BlockSpec(memory_space=pl.ANY)],
        out_specs=(vmem, vmem),
        scratch_shapes=[
            pltpu.VMEM((4 * ks, 256), BF16),
            pltpu.VMEM((4, half, ks), BF16),
            pltpu.VMEM((ks, tokens), BF16),
            pltpu.VMEM((32, width, depth), BF16),
            pltpu.VMEM((tokens, depth), BF16),
            pltpu.VMEM((tokens, kt), BF16),
            pltpu.VMEM((4, 8, 128), F32),
            pltpu.VMEM((2, tokens, cols), F32),
            pltpu.VMEM((2, tokens, cols), BF16),
            pltpu.VMEM((2, 2, tokens, cols), BF16),
            pltpu.VMEM((2, tokens, cols), BF16),
            pltpu.VMEM((2, 2, tokens, cols), BF16),
            pltpu.VMEM((4, 2, tokens, cols), BF16),
            pltpu.VMEM((tokens, ks), F32),
            pltpu.VMEM((ks, cols), F32),
            pltpu.VMEM((4, ks, cols), BF16),
            pltpu.VMEM((4, ks, cols), BF16),
            pltpu.VMEM((4, 16, half, cols), BF16),
            pltpu.VMEM((4, 16, half, cols), BF16),
            pltpu.VMEM((4, half, cols), BF16),
            pltpu.VMEM((2, 2, half, cols), BF16),
            pltpu.SemaphoreType.DMA((SLOTS,)),
            pltpu.SemaphoreType.DMA((SLOTS,)),
            pltpu.SemaphoreType.DMA,
        ],
        compiler_params=pltpu.CompilerParams(
            collective_id=0, has_side_effects=True, vmem_limit_bytes=60 * 2**20
        ),
    )(
        teacher_rows,
        teacher_gain,
        projector.T,
        student_rows,
        student_weight,
    )


def solution(mesh):
    placed = (
        P(("section", "wide"), "narrow"),
        P("narrow"),
        P("narrow", "wide"),
        P(("section", "wide"), "narrow"),
        P(None, "narrow"),
    )
    return jax.shard_map(
        shards,
        mesh=mesh,
        in_specs=placed,
        out_specs=(P(("section", "wide"), "narrow"), P(("section", "wide"), "narrow")),
        check_vma=False,
    )
```

```python
import functools

import jax
import jax.numpy as jnp
from jax import lax
from jax.experimental import pallas as pl
from jax.experimental.pallas import tpu as pltpu
from jax.sharding import PartitionSpec as P

MESH = pl.DeviceIdType.MESH
F32 = jnp.float32
BF16 = jnp.bfloat16

GATHER = 0
ZSWAP = 40
WEIGHT = 41
SQUARES = 45
PAIRED = 48
SIBLING = 49
NARROW_RS = 51
NARROW_AG = 57
CORE_SUM = 65
WIDE_RS = 70
FINAL = 75
SLOTS = 79


def kernel(
    t_ref, g_ref, pt_ref, x_ref, weight_ref, ig_ref, wg_ref, window, wt_ref, xt_ref,
    ct, lhs, hid, sq, inverse, part, far_out, near_out, far_in, near_in, m, igacc,
    kept, core_out, core_in, wide_out, wide_in, fin_out, fin_in, send_sem, recv_sem, local_sem,
):
    c = lax.axis_index("section")
    w = lax.axis_index("wide")
    n = lax.axis_index("narrow")
    x, y, zl = w % 4, (w // 4) % 4, w // 16
    tokens, kt = t_ref.shape
    ks = x_ref.shape[1]
    half = pt_ref.shape[0] // 2
    depth = kt + ks
    cut = (depth // 256 + 1) * 128
    cols = ks // 2
    rows = pl.ds(pl.multiple_of(half * c, half), half)

    def at(zz, yy, xx):
        return zz * 16 + yy * 4 + xx

    sibling = {"section": 1 - c}
    z_other = {"wide": at(1 - zl, y, x)}
    n_dev = [None] + [{"narrow": (n + d) % 4} for d in (1, 2, 3)]

    def peer(k):
        return (y + k // 4) % 4, (x + k % 4) % 4

    def target(d):
        return {"section": n // 2, "wide": at(n % 2, y, x), "narrow": (n + d) % 4}

    at_home = n == 2 * c + zl
    sources = [
        ({"section": cc, "wide": at(zz, y, x), "narrow": 2 * c + zl}, jnp.logical_and(at_home, jnp.logical_and(cc == c, zz == zl)))
        for zz in range(2)
        for cc in range(2)
    ]

    holder = n % 2 == y // 2
    w_slab = at(n // 2, y, x)
    column = 2 * half * (w % 8) + half * c
    low = jnp.minimum(column // 128 * 128, ks - 256)
    fetch = pltpu.make_async_copy(weight_ref.at[:, pl.ds(pl.multiple_of(low, 128), 256)], window, local_sem)

    @pl.when(holder)
    def _():
        fetch.start()

    barrier = pltpu.get_barrier_semaphore()
    greeted = [sibling, z_other, n_dev[1], n_dev[2], n_dev[3]]
    for device in greeted:
        pl.semaphore_signal(barrier, inc=1, device_id=device, device_id_type=MESH)

    def greet(k, carry):
        yy, xx = peer(k)
        pl.semaphore_signal(barrier, inc=1, device_id={"wide": at(zl, yy, xx)}, device_id_type=MESH)
        return carry

    lax.fori_loop(1, 16, greet, 0)
    for device, mine in sources:

        @pl.when(jnp.logical_not(mine))
        def _():
            pl.semaphore_signal(barrier, inc=1, device_id=device, device_id_type=MESH)

    pl.semaphore_wait(barrier, jnp.where(at_home, len(greeted) + 18, len(greeted) + 19))

    def copy(src, dst, slot, device):
        return pltpu.make_async_remote_copy(
            src_ref=src, dst_ref=dst, send_sem=send_sem.at[slot], recv_sem=recv_sem.at[slot],
            device_id=device, device_id_type=MESH,
        )

    w_cols, p_cols = pl.ds(kt, ks), pl.ds(0, kt)

    def weight_copy(k, plane):
        return pltpu.make_async_remote_copy(
            src_ref=wt_ref.at[(n + k) % 4], dst_ref=ct.at[w_slab, rows, w_cols], send_sem=send_sem.at[WEIGHT + k],
            recv_sem=recv_sem.at[WEIGHT + plane], device_id=n_dev[k], device_id_type=MESH,
        )

    ct[w, rows, p_cols] = pt_ref[rows, :]
    z_copy = copy(ct.at[w, rows, p_cols], ct.at[w, rows, p_cols], ZSWAP, z_other)
    z_copy.start()

    @pl.when(holder)
    def _():
        fetch.wait()
        row = lax.broadcasted_iota(jnp.int32, (half, 256), 0)
        lane = lax.broadcasted_iota(jnp.int32, (half, 256), 1)
        pick = jnp.where(lane == row + (column - low), 1.0, 0.0).astype(BF16)

        def transpose(q, carry):
            span = pl.ds(pl.multiple_of(ks * q, ks), ks)
            wt_ref[q] = lax.dot_general(
                pick, window[span, :], (((1,), (1,)), ((), ())), preferred_element_type=F32
            ).astype(BF16)
            return carry

        lax.fori_loop(0, 4, transpose, 0)
        for k in (2, 1, 3):
            weight_copy(k, n // 2).start()
        ct[w_slab, rows, w_cols] = wt_ref[n]

    def weight_arrives(plane):
        @pl.when(n != 2 * plane + y // 2)
        def _():
            weight_copy(1, plane).wait_recv()

        @pl.when(zl != plane)
        def _():
            z_copy.wait_recv()

    def slab(index, part=None):
        if part is None:
            return ct.at[index, rows]
        return ct.at[index, rows, pl.ds(0, cut) if part == 0 else pl.ds(cut, depth - cut)]

    def spread(index, slot, device, part=None):
        return copy(slab(index, part), slab(index, part), slot, device)

    def start(item):
        item.start()

    along_a, along_b = jnp.where(c == 0, x, y), jnp.where(c == 0, y, x)

    def cell(plane, da, db):
        a, b = (along_a + da) % 4, (along_b + db) % 4
        return plane * 16 + jnp.where(c == 0, 4 * b + a, 4 * a + b)

    first = [{"wide": cell(zl, 1, 0)}, {"wide": cell(zl, 3, 0)}, {"wide": cell(zl, 2, 0)}]
    second = [{"wide": cell(zl, 0, 1)}, {"wide": cell(zl, 0, 3)}]
    ALONG = (0, 3, 1, 2)

    class Plane:
        def __init__(self, p, plane):
            self.base, self.p, self.plane = GATHER + 20 * p, p, plane

        def to_sibling(self, index):
            copy(slab(index), slab(index), SIBLING + self.p, sibling).start()

        def whole(self):
            planes = ct.at[pl.ds(16 * self.plane, 16), rows]
            return copy(planes, planes, SIBLING + self.p, sibling)

        def begin(self):
            weight_arrives(self.plane)
            own = cell(self.plane, 0, 0)
            for side in range(3):
                start(spread(own, self.base + side, first[side]))
            self.second_send(0)
            self.to_sibling(own)

        def second_send(self, j):
            index = cell(self.plane, ALONG[j], 0)
            for side in range(2):
                start(spread(index, self.base + 4 + 4 * j + side, second[side]))

        def first_near(self):
            for side in range(2):
                index = cell(self.plane, ALONG[1 + side], 0)
                spread(index, self.base + side, first[side]).wait_recv()
                self.second_send(1 + side)
                self.to_sibling(index)

        def first_far(self):
            index = cell(self.plane, 2, 0)
            spread(index, self.base + 2, first[2]).wait_recv()
            self.second_send(3)
            self.to_sibling(index)

        def second_near(self, j):
            slot = self.base + 4 + 4 * j
            for side in range(2):
                index = cell(self.plane, ALONG[j], 3 if side == 0 else 1)
                spread(index, slot + side, second[side]).wait_recv()
                start(spread(index, slot + 2 + side, second[side], side))
                self.to_sibling(index)

        def second_far(self, j):
            slot = self.base + 4 + 4 * j
            index = cell(self.plane, ALONG[j], 2)
            for side in range(2):
                spread(index, slot + 2 + side, second[side], side).wait_recv()
            self.to_sibling(index)

        def wait_sends(self):
            for side in range(3):
                spread(0, self.base + side, first[0]).wait_send()
            for j in range(4):
                for side in range(2):
                    spread(0, self.base + 4 + 4 * j + side, first[0]).wait_send()
                    spread(0, self.base + 6 + 4 * j + side, first[0], side).wait_send()

    p_first = 1 - n // 2
    near_plane, far_plane = Plane(0, p_first), Plane(1, 1 - p_first)
    near_plane.begin()

    eye = lax.broadcasted_iota(jnp.int32, (128, 128), 0) == lax.broadcasted_iota(jnp.int32, (128, 128), 1)
    groups = tokens // 128
    sq[0] = jnp.zeros((8, 128), F32)

    def squares(i, carry):
        part_t = t_ref[pl.ds(pl.multiple_of(128 * i, 128), 128), :].astype(F32)
        col = jnp.sum(part_t * part_t, axis=1, keepdims=True)
        sq[0, pl.ds(i, 1), :] = jnp.sum(jnp.where(eye, col, 0.0), axis=0, keepdims=True)
        return carry

    lax.fori_loop(0, groups, squares, 0)
    sq_copies = [copy(sq.at[0], sq.at[d], SQUARES + d - 1, n_dev[d]) for d in (1, 2, 3)]
    for item in sq_copies:
        item.start()

    for item in sq_copies:
        item.wait_recv()
    inverse[...] = lax.rsqrt((sq[0] + sq[1] + sq[2] + sq[3]) / (4 * kt) + 1e-05)

    def normalize(i, carry):
        span = pl.ds(pl.multiple_of(128 * i, 128), 128)
        col = jnp.sum(jnp.where(eye, inverse[pl.ds(i, 1), :], 0.0), axis=1, keepdims=True)
        gain = g_ref[...].astype(F32).reshape(1, kt)
        hid[span, :] = -(t_ref[span, :].astype(F32) * col * gain).astype(BF16)
        lhs[span, pl.ds(kt, ks)] = x_ref[span, :]
        xt_ref[:, span] = x_ref[span, :].T
        return carry

    lax.fori_loop(0, groups, normalize, 0)
    paired_copy = copy(hid, lhs.at[:, pl.ds(0, kt)], PAIRED, sibling)
    paired_copy.start()

    near_plane.first_near()
    near_plane.second_near(0)
    near_plane.first_far()
    near_plane.second_near(1)
    near_plane.second_far(0)
    far_plane.begin()
    near_plane.second_near(2)
    near_plane.second_far(1)
    near_plane.second_near(3)
    far_plane.first_near()
    near_plane.second_far(2)
    near_plane.second_far(3)
    paired_copy.wait_recv()
    near_plane.whole().wait_recv()

    e2 = n % 2
    e1 = 1 - e2

    def by(e):
        return {"narrow": (n + 1 + 2 * e) % 4}

    def far_copy(e):
        return copy(far_out.at[e], far_in.at[e], NARROW_RS + e, by(e))

    def early_copy(e):
        return copy(near_out.at[e, 1 - e], near_in.at[e, 1 - e], NARROW_RS + 2 + e, by(e))

    def late_copy(e):
        return copy(near_out.at[e, e], near_in.at[e, e], NARROW_RS + 4 + e, by(e))

    def product(b, h):
        block = ct[pl.ds(8 * b + 4 * h, 4)].reshape(cols, depth)
        return lax.dot_general(lhs[...], block, (((1,), (1,)), ((), ())), preferred_element_type=F32)

    def send_late(e):
        far_copy(e).wait_recv()
        near_out[e, e] = (part[e] + far_in[e].astype(F32)).astype(BF16)
        late_copy(e).start()

    def products(i, carry):
        r, k = i // 2, i % 2

        @pl.when(i == 2)
        def _():
            far_plane.second_near(0)
            far_plane.first_far()

        @pl.when(i == 4)
        def _():
            far_plane.second_near(1)
            far_plane.second_far(0)
            far_plane.second_near(2)
            far_plane.second_far(1)
            far_plane.second_near(3)

        @pl.when(jnp.logical_or(i == 4, i == 6))
        def _():
            send_late(jnp.where(i == 4, e1, e2))

        @pl.when(i == 4)
        def _():
            far_plane.second_far(2)
            far_plane.second_far(3)
            far_plane.whole().wait_recv()

        e = jnp.where(r == 1, e1, e2)
        beside = jnp.logical_or(r == 1, r == 2)
        b = (n + jnp.where(r == 0, 2, jnp.where(r == 3, 0, 1 + 2 * e))) % 4
        h = jnp.where(beside, jnp.where(k == 0, 1 - e, e), k)
        early = jnp.logical_and(beside, k == 0)
        part[h] = product(b, h)

        @pl.when(r == 0)
        def _():
            far_out[k] = part[h].astype(BF16)
            far_copy(k).start()

        @pl.when(early)
        def _():
            near_out[e, h] = part[h].astype(BF16)
            early_copy(e).start()

        return carry

    lax.fori_loop(0, 8, products, 0)


    def own_copy(h, e):
        return copy(m.at[n, h], m.at[n, h], NARROW_AG + 2 * e + h, by(e))

    def pass_on(e):
        piece = m.at[(n + 3 + 2 * e) % 4, e]
        return copy(piece, piece, NARROW_AG + 4 + e, by(e))

    early_copy(e2).wait_recv()
    late_copy(e2).wait_recv()

    def finish(k, carry):
        h = jnp.where(k == 0, 1 - e1, e1)

        @pl.when(k == 0)
        def _():
            early_copy(e1).wait_recv()

        @pl.when(k == 1)
        def _():
            late_copy(e1).wait_recv()

        span = pl.ds(pl.multiple_of(cols * h, cols), cols)
        own = part[h] + x_ref[:, span].astype(F32)
        m[n, h] = (own + near_in[0, h].astype(F32) + near_in[1, h].astype(F32)).astype(BF16)
        own_copy(h, 0).start()
        own_copy(h, 1).start()
        return carry

    lax.fori_loop(0, 2, finish, 0)
    igacc[...] = jnp.zeros((tokens, ks), F32)
    me = 4 * y + x

    def core_copy(d):
        return copy(core_out.at[d], core_in.at[d], CORE_SUM + d, sibling)

    def wide_send(d):
        def one(k, carry):
            yy, xx = peer(k)
            copy(
                wide_out.at[d, 4 * yy + xx], wide_in.at[d, me], WIDE_RS + d, {"wide": at(zl, yy, xx)}
            ).start()
            return carry

        lax.fori_loop(1, 16, one, 0)

    def wide_all(d):
        return copy(
            wide_out.at[d, pl.ds(0, 15)], wide_in.at[d, pl.ds(0, 15)], WIDE_RS + d, {"wide": at(zl, y, (x + 1) % 4)}
        )

    def chip_sum(d):
        core_copy(d).wait_recv()
        both = (kept[...] + core_in[d].astype(F32)).astype(BF16)
        wide_out[d] = both.reshape(16, half, cols)
        wide_in[d, me] = wide_out[d, me]
        wide_send(d)

    def final_copy(d):
        return pltpu.make_async_remote_copy(
            src_ref=fin_out.at[d], dst_ref=fin_in.at[zl, c], send_sem=send_sem.at[FINAL + d],
            recv_sem=recv_sem.at[FINAL + 2 * zl + c], device_id=target(d), device_id_type=MESH,
        )

    def reduce(d):
        wide_all(d).wait_recv()
        total = wide_in[d, 0].astype(F32)
        for k in range(1, 16):
            total = total + wide_in[d, k].astype(F32)
        stays = jnp.logical_and(at_home, d == 0)

        @pl.when(stays)
        def _():
            fin_in[zl, c] = total.astype(BF16)

        @pl.when(jnp.logical_not(stays))
        def _():
            fin_out[d] = total.astype(BF16)
            final_copy(d).start()

    def backward(i, carry):
        @pl.when(i == 2)
        def _():
            own_copy(0, 0).wait_recv()
            pass_on(0).start()
            own_copy(1, 1).wait_recv()
            pass_on(1).start()
            own_copy(1, 0).wait_recv()

        @pl.when(i == 4)
        def _():
            own_copy(0, 1).wait_recv()

        @pl.when(i == 6)
        def _():
            early_waits()
            pass_on(0).wait_recv()
            pass_on(1).wait_recv()

        r = i // 2
        d = jnp.where(r == 0, 0, jnp.where(r == 1, 3, jnp.where(r == 2, 1, 2)))
        h = jnp.where(i % 2 == 0, 1 - c, c)
        b = (n + d) % 4
        kept[...] = jnp.dot(xt_ref[...], m[b, h], preferred_element_type=F32)

        @pl.when(i % 2 == 0)
        def _():
            core_out[d] = kept[...].astype(BF16)
            core_copy(d).start()

        block = ct[pl.ds(8 * b + 4 * h, 4), :, pl.ds(kt, ks)].reshape(cols, ks)
        igacc[...] += jnp.dot(m[b, h], block, preferred_element_type=F32)

        @pl.when(i % 2 == 1)
        def _():
            chip_sum(d)

        return carry

    def early_waits():
        for item in sq_copies + [z_copy, paired_copy, near_plane.whole(), far_plane.whole()]:
            item.wait_send()
        near_plane.wait_sends()
        far_plane.wait_sends()
        for e in range(2):
            far_copy(e).wait_send()
            early_copy(e).wait_send()
            late_copy(e).wait_send()

        @pl.when(holder)
        def _():
            for k in range(1, 4):
                weight_copy(k, n // 2).wait_send()

    lax.fori_loop(0, 8, backward, 0)
    for h in range(2):
        span = slice(cols * h, cols * h + cols)
        ig_ref[:, span] = (m[n, h].astype(F32) + igacc[:, span]).astype(BF16)

    def reduce_all(r, carry):
        reduce(jnp.where(r == 1, 3, jnp.where(r == 2, 1, 2 * (r // 3))))
        return carry

    lax.fori_loop(0, 4, reduce_all, 0)

    def late_waits():
        for e in range(2):
            pass_on(e).wait_send()
            for h in range(2):
                own_copy(h, e).wait_send()
        for d in range(4):
            core_copy(d).wait_send()
            wide_all(d).wait_send()

            @pl.when(jnp.logical_not(jnp.logical_and(at_home, d == 0)))
            def _():
                final_copy(d).wait_send()

    scale = 1.0 / (tokens * 64.0) ** 0.5
    for zz in range(2):
        for cc in range(2):

            @pl.when(jnp.logical_not(sources[2 * zz + cc][1]))
            def _():
                pltpu.make_async_remote_copy(
                    src_ref=fin_out.at[0], dst_ref=fin_in.at[zz, cc], send_sem=send_sem.at[FINAL],
                    recv_sem=recv_sem.at[FINAL + 2 * zz + cc], device_id=sibling, device_id_type=MESH,
                ).wait_recv()

    for h in range(2):
        wg_ref[:, cols * h : cols * h + cols] = (fin_in[0, h].astype(F32) + fin_in[1, h].astype(F32)) * scale

    late_waits()


def shards(teacher_rows, teacher_gain, projector, student_rows, student_weight):
    tokens, kt = teacher_rows.shape
    ks = student_rows.shape[1]
    width = projector.shape[1]
    half, cols, depth = width // 2, ks // 2, kt + ks
    vmem = pl.BlockSpec(memory_space=pltpu.VMEM)
    return pl.pallas_call(
        kernel,
        out_shape=(
            jax.ShapeDtypeStruct((tokens, ks), BF16),
            jax.ShapeDtypeStruct((half, ks), F32),
        ),
        in_specs=[vmem] * 4 + [pl.BlockSpec(memory_space=pl.ANY)],
        out_specs=(vmem, vmem),
        scratch_shapes=[
            pltpu.VMEM((4 * ks, 256), BF16),
            pltpu.VMEM((4, half, ks), BF16),
            pltpu.VMEM((ks, tokens), BF16),
            pltpu.VMEM((32, width, depth), BF16),
            pltpu.VMEM((tokens, depth), BF16),
            pltpu.VMEM((tokens, kt), BF16),
            pltpu.VMEM((4, 8, 128), F32),
            pltpu.VMEM((8, 128), F32),
            pltpu.VMEM((2, tokens, cols), F32),
            pltpu.VMEM((2, tokens, cols), BF16),
            pltpu.VMEM((2, 2, tokens, cols), BF16),
            pltpu.VMEM((2, tokens, cols), BF16),
            pltpu.VMEM((2, 2, tokens, cols), BF16),
            pltpu.VMEM((4, 2, tokens, cols), BF16),
            pltpu.VMEM((tokens, ks), F32),
            pltpu.VMEM((ks, cols), F32),
            pltpu.VMEM((4, ks, cols), BF16),
            pltpu.VMEM((4, ks, cols), BF16),
            pltpu.VMEM((4, 16, half, cols), BF16),
            pltpu.VMEM((4, 16, half, cols), BF16),
            pltpu.VMEM((4, half, cols), BF16),
            pltpu.VMEM((2, 2, half, cols), BF16),
            pltpu.SemaphoreType.DMA((SLOTS,)),
            pltpu.SemaphoreType.DMA((SLOTS,)),
            pltpu.SemaphoreType.DMA,
        ],
        compiler_params=pltpu.CompilerParams(
            collective_id=0, has_side_effects=True, vmem_limit_bytes=60 * 2**20
        ),
    )(
        teacher_rows,
        teacher_gain,
        projector.T,
        student_rows,
        student_weight,
    )


def solution(mesh):
    placed = (
        P(("section", "wide"), "narrow"),
        P("narrow"),
        P("narrow", "wide"),
        P(("section", "wide"), "narrow"),
        P(None, "narrow"),
    )
    return jax.shard_map(
        shards,
        mesh=mesh,
        in_specs=placed,
        out_specs=(P(("section", "wide"), "narrow"), P(("section", "wide"), "narrow")),
        check_vma=False,
    )
```

```python
import functools

import jax
import jax.numpy as jnp
from jax import lax
from jax.experimental import pallas as pl
from jax.experimental.pallas import tpu as pltpu
from jax.sharding import PartitionSpec as P

MESH = pl.DeviceIdType.MESH
F32 = jnp.float32
BF16 = jnp.bfloat16

GATHER = 0
ZSWAP = 40
WEIGHT = 41
SQUARES = 45
PAIRED = 48
SIBLING = 49
NARROW_RS = 51
NARROW_AG = 57
CORE_SUM = 67
WIDE_RS = 73
FINAL = 79
SLOTS = 83


def kernel(
    t_ref, g_ref, pt_ref, x_ref, weight_ref, ig_ref, wg_ref, window, wt_ref, xt_ref,
    ct, lhs, hid, sq, inverse, part, far_out, near_out, far_in, near_in, m, igacc,
    kept, core_out, core_in, wide_out, wide_in, tile_out, tile_in, far_wide_out, far_wide_in, fin_out, fin_in, send_sem, recv_sem, local_sem,
):
    c = lax.axis_index("section")
    w = lax.axis_index("wide")
    n = lax.axis_index("narrow")
    x, y, zl = w % 4, (w // 4) % 4, w // 16
    tokens, kt = t_ref.shape
    ks = x_ref.shape[1]
    half = pt_ref.shape[0] // 2
    depth = kt + ks
    cut = (depth // 256 + 1) * 128
    cols = ks // 2
    rows = pl.ds(pl.multiple_of(half * c, half), half)

    def at(zz, yy, xx):
        return zz * 16 + yy * 4 + xx

    sibling = {"section": 1 - c}
    z_other = {"wide": at(1 - zl, y, x)}
    n_dev = [None] + [{"narrow": (n + d) % 4} for d in (1, 2, 3)]

    def peer(k):
        return (y + k // 4) % 4, (x + k % 4) % 4

    def target(d):
        return {"section": n // 2, "wide": at(n % 2, y, x), "narrow": (n + d) % 4}

    at_home = n == 2 * c + zl
    sources = [
        ({"section": cc, "wide": at(zz, y, x), "narrow": 2 * c + zl}, jnp.logical_and(at_home, jnp.logical_and(cc == c, zz == zl)))
        for zz in range(2)
        for cc in range(2)
    ]

    holder = n % 2 == y // 2
    w_slab = at(n // 2, y, x)
    column = 2 * half * (w % 8) + half * c
    low = jnp.minimum(column // 128 * 128, ks - 256)
    fetch = pltpu.make_async_copy(weight_ref.at[:, pl.ds(pl.multiple_of(low, 128), 256)], window, local_sem)

    @pl.when(holder)
    def _():
        fetch.start()

    barrier = pltpu.get_barrier_semaphore()
    greeted = [sibling, z_other, n_dev[1], n_dev[2], n_dev[3]]
    for device in greeted:
        pl.semaphore_signal(barrier, inc=1, device_id=device, device_id_type=MESH)

    def greet(k, carry):
        yy, xx = peer(k)
        pl.semaphore_signal(barrier, inc=1, device_id={"wide": at(zl, yy, xx)}, device_id_type=MESH)
        return carry

    lax.fori_loop(1, 16, greet, 0)
    for device, mine in sources:

        @pl.when(jnp.logical_not(mine))
        def _():
            pl.semaphore_signal(barrier, inc=1, device_id=device, device_id_type=MESH)

    pl.semaphore_wait(barrier, jnp.where(at_home, len(greeted) + 18, len(greeted) + 19))

    def copy(src, dst, slot, device):
        return pltpu.make_async_remote_copy(
            src_ref=src, dst_ref=dst, send_sem=send_sem.at[slot], recv_sem=recv_sem.at[slot],
            device_id=device, device_id_type=MESH,
        )

    w_cols, p_cols = pl.ds(kt, ks), pl.ds(0, kt)

    def weight_copy(k, plane):
        return pltpu.make_async_remote_copy(
            src_ref=wt_ref.at[(n + k) % 4], dst_ref=ct.at[w_slab, rows, w_cols], send_sem=send_sem.at[WEIGHT + k],
            recv_sem=recv_sem.at[WEIGHT + plane], device_id=n_dev[k], device_id_type=MESH,
        )

    ct[w, rows, p_cols] = pt_ref[rows, :]
    z_copy = copy(ct.at[w, rows, p_cols], ct.at[w, rows, p_cols], ZSWAP, z_other)
    z_copy.start()

    @pl.when(holder)
    def _():
        fetch.wait()
        row = lax.broadcasted_iota(jnp.int32, (half, 256), 0)
        lane = lax.broadcasted_iota(jnp.int32, (half, 256), 1)
        pick = jnp.where(lane == row + (column - low), 1.0, 0.0).astype(BF16)

        def transpose(q, carry):
            span = pl.ds(pl.multiple_of(ks * q, ks), ks)
            wt_ref[q] = lax.dot_general(
                pick, window[span, :], (((1,), (1,)), ((), ())), preferred_element_type=F32
            ).astype(BF16)
            return carry

        lax.fori_loop(0, 4, transpose, 0)
        for k in (2, 1, 3):
            weight_copy(k, n // 2).start()
        ct[w_slab, rows, w_cols] = wt_ref[n]

    def weight_arrives(plane):
        @pl.when(n != 2 * plane + y // 2)
        def _():
            weight_copy(1, plane).wait_recv()

        @pl.when(zl != plane)
        def _():
            z_copy.wait_recv()

    def slab(index, part=None):
        if part is None:
            return ct.at[index, rows]
        return ct.at[index, rows, pl.ds(0, cut) if part == 0 else pl.ds(cut, depth - cut)]

    def spread(index, slot, device, part=None):
        return copy(slab(index, part), slab(index, part), slot, device)

    def start(item):
        item.start()

    along_a, along_b = jnp.where(c == 0, x, y), jnp.where(c == 0, y, x)

    def cell(plane, da, db):
        a, b = (along_a + da) % 4, (along_b + db) % 4
        return plane * 16 + jnp.where(c == 0, 4 * b + a, 4 * a + b)

    first = [{"wide": cell(zl, 1, 0)}, {"wide": cell(zl, 3, 0)}, {"wide": cell(zl, 2, 0)}]
    second = [{"wide": cell(zl, 0, 1)}, {"wide": cell(zl, 0, 3)}]
    ALONG = (0, 3, 1, 2)

    class Plane:
        def __init__(self, p, plane):
            self.base, self.p, self.plane = GATHER + 20 * p, p, plane

        def to_sibling(self, index):
            copy(slab(index), slab(index), SIBLING + self.p, sibling).start()

        def whole(self):
            planes = ct.at[pl.ds(16 * self.plane, 16), rows]
            return copy(planes, planes, SIBLING + self.p, sibling)

        def begin(self):
            weight_arrives(self.plane)
            own = cell(self.plane, 0, 0)
            for side in range(3):
                start(spread(own, self.base + side, first[side]))
            self.second_send(0)
            self.to_sibling(own)

        def second_send(self, j):
            index = cell(self.plane, ALONG[j], 0)
            for side in range(2):
                start(spread(index, self.base + 4 + 4 * j + side, second[side]))

        def first_near(self):
            for side in range(2):
                index = cell(self.plane, ALONG[1 + side], 0)
                spread(index, self.base + side, first[side]).wait_recv()
                self.second_send(1 + side)
                self.to_sibling(index)

        def first_far(self):
            index = cell(self.plane, 2, 0)
            spread(index, self.base + 2, first[2]).wait_recv()
            self.second_send(3)
            self.to_sibling(index)

        def second_near(self, j):
            slot = self.base + 4 + 4 * j
            for side in range(2):
                index = cell(self.plane, ALONG[j], 3 if side == 0 else 1)
                spread(index, slot + side, second[side]).wait_recv()
                start(spread(index, slot + 2 + side, second[side], side))
                self.to_sibling(index)

        def second_far(self, j):
            slot = self.base + 4 + 4 * j
            index = cell(self.plane, ALONG[j], 2)
            for side in range(2):
                spread(index, slot + 2 + side, second[side], side).wait_recv()
            self.to_sibling(index)

        def wait_sends(self):
            for side in range(3):
                spread(0, self.base + side, first[0]).wait_send()
            for j in range(4):
                for side in range(2):
                    spread(0, self.base + 4 + 4 * j + side, first[0]).wait_send()
                    spread(0, self.base + 6 + 4 * j + side, first[0], side).wait_send()

    p_first = 1 - n // 2
    near_plane, far_plane = Plane(0, p_first), Plane(1, 1 - p_first)
    near_plane.begin()

    eye = lax.broadcasted_iota(jnp.int32, (128, 128), 0) == lax.broadcasted_iota(jnp.int32, (128, 128), 1)
    groups = tokens // 128
    sq[0] = jnp.zeros((8, 128), F32)

    def squares(i, carry):
        part_t = t_ref[pl.ds(pl.multiple_of(128 * i, 128), 128), :].astype(F32)
        col = jnp.sum(part_t * part_t, axis=1, keepdims=True)
        sq[0, pl.ds(i, 1), :] = jnp.sum(jnp.where(eye, col, 0.0), axis=0, keepdims=True)
        return carry

    lax.fori_loop(0, groups, squares, 0)
    sq_copies = [copy(sq.at[0], sq.at[d], SQUARES + d - 1, n_dev[d]) for d in (1, 2, 3)]
    for item in sq_copies:
        item.start()

    for item in sq_copies:
        item.wait_recv()
    inverse[...] = lax.rsqrt((sq[0] + sq[1] + sq[2] + sq[3]) / (4 * kt) + 1e-05)

    def normalize(i, carry):
        span = pl.ds(pl.multiple_of(128 * i, 128), 128)
        col = jnp.sum(jnp.where(eye, inverse[pl.ds(i, 1), :], 0.0), axis=1, keepdims=True)
        gain = g_ref[...].astype(F32).reshape(1, kt)
        hid[span, :] = -(t_ref[span, :].astype(F32) * col * gain).astype(BF16)
        lhs[span, pl.ds(kt, ks)] = x_ref[span, :]
        xt_ref[:, span] = x_ref[span, :].T
        return carry

    lax.fori_loop(0, groups, normalize, 0)
    paired_copy = copy(hid, lhs.at[:, pl.ds(0, kt)], PAIRED, sibling)
    paired_copy.start()

    near_plane.first_near()
    near_plane.second_near(0)
    near_plane.first_far()
    near_plane.second_near(1)
    near_plane.second_far(0)
    far_plane.begin()
    near_plane.second_near(2)
    near_plane.second_far(1)
    near_plane.second_near(3)
    far_plane.first_near()
    near_plane.second_far(2)
    near_plane.second_far(3)
    paired_copy.wait_recv()
    near_plane.whole().wait_recv()

    e2 = n % 2
    e1 = 1 - e2

    def by(e):
        return {"narrow": (n + 1 + 2 * e) % 4}

    def far_copy(e):
        return copy(far_out.at[e], far_in.at[e], NARROW_RS + e, by(e))

    def early_copy(e):
        return copy(near_out.at[e, 1 - e], near_in.at[e, 1 - e], NARROW_RS + 2 + e, by(e))

    def late_copy(e):
        return copy(near_out.at[e, e], near_in.at[e, e], NARROW_RS + 4 + e, by(e))

    def product(b, h):
        block = ct[pl.ds(8 * b + 4 * h, 4)].reshape(cols, depth)
        return lax.dot_general(lhs[...], block, (((1,), (1,)), ((), ())), preferred_element_type=F32)

    def send_late(e):
        far_copy(e).wait_recv()
        near_out[e, e] = (part[e] + far_in[e].astype(F32)).astype(BF16)
        late_copy(e).start()

    def products(i, carry):
        r, k = i // 2, i % 2

        @pl.when(i == 2)
        def _():
            far_plane.second_near(0)
            far_plane.first_far()

        @pl.when(i == 4)
        def _():
            far_plane.second_near(1)
            far_plane.second_far(0)
            far_plane.second_near(2)
            far_plane.second_far(1)
            far_plane.second_near(3)

        @pl.when(jnp.logical_or(i == 4, i == 6))
        def _():
            send_late(jnp.where(i == 4, e1, e2))

        @pl.when(i == 4)
        def _():
            far_plane.second_far(2)
            far_plane.second_far(3)
            far_plane.whole().wait_recv()

        e = jnp.where(r == 1, e1, e2)
        beside = jnp.logical_or(r == 1, r == 2)
        b = (n + jnp.where(r == 0, 2, jnp.where(r == 3, 0, 1 + 2 * e))) % 4
        h = jnp.where(beside, jnp.where(k == 0, 1 - e, e), k)
        early = jnp.logical_and(beside, k == 0)
        part[h] = product(b, h)

        @pl.when(r == 0)
        def _():
            far_out[k] = part[h].astype(BF16)
            far_copy(k).start()

        @pl.when(early)
        def _():
            near_out[e, h] = part[h].astype(BF16)
            early_copy(e).start()

        return carry

    lax.fori_loop(0, 8, products, 0)

    tiles = cols // 128

    def own_copy(h, e):
        return copy(m.at[n, h], m.at[n, h], NARROW_AG + 2 * e + h, by(e))

    def pass_on(e, j):
        piece = m.at[(n + 3 + 2 * e) % 4, e, j]
        return copy(piece, piece, NARROW_AG + 4 + tiles * e + j, by(e))

    def pass_all(e):
        def one(j, carry):
            pass_on(e, j).start()
            return carry

        lax.fori_loop(0, tiles, one, 0)

    def whole(b, h):
        return jnp.concatenate([m[b, h, j] for j in range(tiles)], axis=1)

    early_copy(e2).wait_recv()
    late_copy(e2).wait_recv()

    def finish(k, carry):
        h = jnp.where(k == 0, 1 - e1, e1)

        @pl.when(k == 0)
        def _():
            early_copy(e1).wait_recv()

        @pl.when(k == 1)
        def _():
            late_copy(e1).wait_recv()

        span = pl.ds(pl.multiple_of(cols * h, cols), cols)
        own = part[h] + x_ref[:, span].astype(F32)
        total = (own + near_in[0, h].astype(F32) + near_in[1, h].astype(F32)).astype(BF16)
        for j in range(tiles):
            m[n, h, j] = total[:, 128 * j : 128 * j + 128]
        own_copy(h, 0).start()
        own_copy(h, 1).start()
        return carry

    lax.fori_loop(0, 2, finish, 0)
    igacc[...] = jnp.zeros((tokens, ks), F32)
    me = 4 * y + x

    def core_copy(slot):
        return copy(core_out.at[slot], core_in.at[slot], CORE_SUM + slot, sibling)

    def core_tile(j):
        return copy(tile_out.at[j], tile_in.at[j], CORE_SUM + 3 + j, sibling)

    def wide_send(out, into, slot):
        def one(k, carry):
            yy, xx = peer(k)
            copy(out.at[4 * yy + xx], into.at[me], slot, {"wide": at(zl, yy, xx)}).start()
            return carry

        lax.fori_loop(1, 16, one, 0)

    def wide_all(out, into, slot):
        return copy(out.at[pl.ds(0, 15)], into.at[pl.ds(0, 15)], slot, {"wide": at(zl, y, (x + 1) % 4)})

    def wide_block(slot):
        return wide_all(wide_out.at[slot], wide_in.at[slot], WIDE_RS + slot)

    def wide_tile(j):
        return wide_all(far_wide_out.at[j], far_wide_in.at[j], WIDE_RS + 3 + j)

    def chip_sum(slot):
        core_copy(slot).wait_recv()
        both = (kept[...] + core_in[slot].astype(F32)).astype(BF16)
        wide_out[slot] = both.reshape(16, half, cols)
        wide_in[slot, me] = wide_out[slot, me]
        wide_send(wide_out.at[slot], wide_in.at[slot], WIDE_RS + slot)

    def final_copy(d):
        return pltpu.make_async_remote_copy(
            src_ref=fin_out.at[d], dst_ref=fin_in.at[zl, c], send_sem=send_sem.at[FINAL + d],
            recv_sem=recv_sem.at[FINAL + 2 * zl + c], device_id=target(d), device_id_type=MESH,
        )

    def reduce(slot):
        d = jnp.where(slot == 2, 3, slot)
        wide_block(slot).wait_recv()
        total = wide_in[slot, 0].astype(F32)
        for k in range(1, 16):
            total = total + wide_in[slot, k].astype(F32)
        stays = jnp.logical_and(at_home, d == 0)

        @pl.when(stays)
        def _():
            fin_in[zl, c] = total.astype(BF16)

        @pl.when(jnp.logical_not(stays))
        def _():
            fin_out[d] = total.astype(BF16)
            final_copy(d).start()

    def add_input_grad(b, h):
        block = ct[pl.ds(8 * b + 4 * h, 4), :, pl.ds(kt, ks)].reshape(cols, ks)
        igacc[...] += jnp.dot(whole(b, h), block, preferred_element_type=F32)

    soon = 1 - n % 2

    def backward(i, carry):
        @pl.when(jnp.logical_or(i == 2, i == 4))
        def _():
            arrived = jnp.where(i == 2, soon, 1 - soon)
            own_copy(arrived, arrived).wait_recv()
            pass_all(arrived)
            own_copy(arrived, 1 - arrived).wait_recv()

        d = jnp.where(i < 2, 0, jnp.where(i % 2 == 0, 3, 1))
        h = jnp.where(i == 0, 1 - c, jnp.where(i == 1, c, jnp.where(i < 4, soon, 1 - soon)))
        slot = jnp.where(d == 3, 2, d)
        b = (n + d) % 4
        kept[...] = jnp.dot(xt_ref[...], whole(b, h), preferred_element_type=F32)

        @pl.when(h != c)
        def _():
            core_out[slot] = kept[...].astype(BF16)
            core_copy(slot).start()

        add_input_grad(b, h)

        @pl.when(h == c)
        def _():
            chip_sum(slot)

        return carry

    def far_gradient(j, carry):
        b = (n + 2) % 4
        for e in range(2):
            pass_on(e, j).wait_recv()
        tile_out[j] = jnp.dot(xt_ref[...], m[b, 1 - c, j], preferred_element_type=F32).astype(BF16)
        core_tile(j).start()
        own = jnp.dot(xt_ref[...], m[b, c, j], preferred_element_type=F32)
        core_tile(j).wait_recv()
        far_wide_out[j] = (own + tile_in[j].astype(F32)).astype(BF16).reshape(16, half, 128)
        far_wide_in[j, me] = far_wide_out[j, me]
        wide_send(far_wide_out.at[j], far_wide_in.at[j], WIDE_RS + 3 + j)
        return carry

    def early_waits():
        for item in sq_copies + [z_copy, paired_copy, near_plane.whole(), far_plane.whole()]:
            item.wait_send()
        near_plane.wait_sends()
        far_plane.wait_sends()
        for e in range(2):
            far_copy(e).wait_send()
            early_copy(e).wait_send()
            late_copy(e).wait_send()

        @pl.when(holder)
        def _():
            for k in range(1, 4):
                weight_copy(k, n // 2).wait_send()

    def early_sums(slot, carry):
        reduce(slot)
        return carry

    def last_input_grad(h, carry):
        add_input_grad((n + 2) % 4, h)
        return carry

    lax.fori_loop(0, 6, backward, 0)
    early_waits()
    lax.fori_loop(0, tiles, far_gradient, 0)
    lax.fori_loop(0, 2, last_input_grad, 0)
    for h in range(2):
        span = slice(cols * h, cols * h + cols)
        ig_ref[:, span] = (whole(n, h).astype(F32) + igacc[:, span]).astype(BF16)

    lax.fori_loop(0, 3, early_sums, 0)
    for j in range(tiles):
        wide_tile(j).wait_recv()
        total = far_wide_in[j, 0].astype(F32)
        for k in range(1, 16):
            total = total + far_wide_in[j, k].astype(F32)
        fin_out[2, :, 128 * j : 128 * j + 128] = total.astype(BF16)
    final_copy(2).start()

    def late_waits():
        for e in range(2):
            for j in range(tiles):
                pass_on(e, j).wait_send()
            for h in range(2):
                own_copy(h, e).wait_send()
        for k in range(3):
            core_copy(k).wait_send()
            core_tile(k).wait_send()
            wide_block(k).wait_send()
            wide_tile(k).wait_send()
        for d in range(4):

            @pl.when(jnp.logical_not(jnp.logical_and(at_home, d == 0)))
            def _():
                final_copy(d).wait_send()

    scale = 1.0 / (tokens * 64.0) ** 0.5
    for zz in range(2):
        for cc in range(2):

            @pl.when(jnp.logical_not(sources[2 * zz + cc][1]))
            def _():
                pltpu.make_async_remote_copy(
                    src_ref=fin_out.at[0], dst_ref=fin_in.at[zz, cc], send_sem=send_sem.at[FINAL],
                    recv_sem=recv_sem.at[FINAL + 2 * zz + cc], device_id=sibling, device_id_type=MESH,
                ).wait_recv()

    for h in range(2):
        wg_ref[:, cols * h : cols * h + cols] = (fin_in[0, h].astype(F32) + fin_in[1, h].astype(F32)) * scale

    late_waits()


def shards(teacher_rows, teacher_gain, projector, student_rows, student_weight):
    tokens, kt = teacher_rows.shape
    ks = student_rows.shape[1]
    width = projector.shape[1]
    half, cols, depth = width // 2, ks // 2, kt + ks
    vmem = pl.BlockSpec(memory_space=pltpu.VMEM)
    return pl.pallas_call(
        kernel,
        out_shape=(
            jax.ShapeDtypeStruct((tokens, ks), BF16),
            jax.ShapeDtypeStruct((half, ks), F32),
        ),
        in_specs=[vmem] * 4 + [pl.BlockSpec(memory_space=pl.ANY)],
        out_specs=(vmem, vmem),
        scratch_shapes=[
            pltpu.VMEM((4 * ks, 256), BF16),
            pltpu.VMEM((4, half, ks), BF16),
            pltpu.VMEM((ks, tokens), BF16),
            pltpu.VMEM((32, width, depth), BF16),
            pltpu.VMEM((tokens, depth), BF16),
            pltpu.VMEM((tokens, kt), BF16),
            pltpu.VMEM((4, 8, 128), F32),
            pltpu.VMEM((8, 128), F32),
            pltpu.VMEM((2, tokens, cols), F32),
            pltpu.VMEM((2, tokens, cols), BF16),
            pltpu.VMEM((2, 2, tokens, cols), BF16),
            pltpu.VMEM((2, tokens, cols), BF16),
            pltpu.VMEM((2, 2, tokens, cols), BF16),
            pltpu.VMEM((4, 2, cols // 128, tokens, 128), BF16),
            pltpu.VMEM((tokens, ks), F32),
            pltpu.VMEM((ks, cols), F32),
            pltpu.VMEM((3, ks, cols), BF16),
            pltpu.VMEM((3, ks, cols), BF16),
            pltpu.VMEM((3, 16, half, cols), BF16),
            pltpu.VMEM((3, 16, half, cols), BF16),
            pltpu.VMEM((3, ks, 128), BF16),
            pltpu.VMEM((3, ks, 128), BF16),
            pltpu.VMEM((3, 16, half, 128), BF16),
            pltpu.VMEM((3, 16, half, 128), BF16),
            pltpu.VMEM((4, half, cols), BF16),
            pltpu.VMEM((2, 2, half, cols), BF16),
            pltpu.SemaphoreType.DMA((SLOTS,)),
            pltpu.SemaphoreType.DMA((SLOTS,)),
            pltpu.SemaphoreType.DMA,
        ],
        compiler_params=pltpu.CompilerParams(
            collective_id=0, has_side_effects=True, vmem_limit_bytes=60 * 2**20
        ),
    )(
        teacher_rows,
        teacher_gain,
        projector.T,
        student_rows,
        student_weight,
    )


def solution(mesh):
    placed = (
        P(("section", "wide"), "narrow"),
        P("narrow"),
        P("narrow", "wide"),
        P(("section", "wide"), "narrow"),
        P(None, "narrow"),
    )
    return jax.shard_map(
        shards,
        mesh=mesh,
        in_specs=placed,
        out_specs=(P(("section", "wide"), "narrow"), P(("section", "wide"), "narrow")),
        check_vma=False,
    )
```

```python
import functools

import jax
import jax.numpy as jnp
from jax import lax
from jax.experimental import pallas as pl
from jax.experimental.pallas import tpu as pltpu
from jax.sharding import PartitionSpec as P

MESH = pl.DeviceIdType.MESH
F32 = jnp.float32
BF16 = jnp.bfloat16

GATHER = 0
ZSWAP = 40
WEIGHT = 41
SQUARES = 45
PAIRED = 48
SIBLING = 49
NARROW_RS = 51
NARROW_AG = 57
CORE_SUM = 67
WIDE_RS = 73
FINAL = 79
SLOTS = 83


def kernel(
    t_ref, g_ref, pt_ref, x_ref, weight_ref, ig_ref, wg_ref, window, wt_ref, xt_ref,
    ct, lhs, hid, sq, inverse, part, far_out, near_out, far_in, near_in, m, igacc,
    kept, core_out, core_in, wide_out, wide_in, tile_out, tile_in, far_wide_out, far_wide_in, fin_out, fin_in, send_sem, recv_sem, local_sem,
):
    c = lax.axis_index("section")
    w = lax.axis_index("wide")
    n = lax.axis_index("narrow")
    x, y, zl = w % 4, (w // 4) % 4, w // 16
    tokens, kt = t_ref.shape
    ks = x_ref.shape[1]
    half = pt_ref.shape[0] // 2
    depth = kt + ks
    cut = (depth // 256 + 1) * 128
    cols = ks // 2
    rows = pl.ds(pl.multiple_of(half * c, half), half)

    def at(zz, yy, xx):
        return zz * 16 + yy * 4 + xx

    sibling = {"section": 1 - c}
    z_other = {"wide": at(1 - zl, y, x)}
    n_dev = [None] + [{"narrow": (n + d) % 4} for d in (1, 2, 3)]

    def peer(k):
        return (y + k // 4) % 4, (x + k % 4) % 4

    def target(d):
        return {"section": n // 2, "wide": at(n % 2, y, x), "narrow": (n + d) % 4}

    at_home = n == 2 * c + zl
    sources = [
        ({"section": cc, "wide": at(zz, y, x), "narrow": 2 * c + zl}, jnp.logical_and(at_home, jnp.logical_and(cc == c, zz == zl)))
        for zz in range(2)
        for cc in range(2)
    ]

    holder = n % 2 == y // 2
    w_slab = at(n // 2, y, x)
    column = 2 * half * (w % 8) + half * c
    low = jnp.minimum(column // 128 * 128, ks - 256)
    fetch = pltpu.make_async_copy(weight_ref.at[:, pl.ds(pl.multiple_of(low, 128), 256)], window, local_sem)

    @pl.when(holder)
    def _():
        fetch.start()

    barrier = pltpu.get_barrier_semaphore()
    greeted = [sibling, z_other, n_dev[1], n_dev[2], n_dev[3]]
    for device in greeted:
        pl.semaphore_signal(barrier, inc=1, device_id=device, device_id_type=MESH)

    def greet(k, carry):
        yy, xx = peer(k)
        pl.semaphore_signal(barrier, inc=1, device_id={"wide": at(zl, yy, xx)}, device_id_type=MESH)
        return carry

    lax.fori_loop(1, 16, greet, 0)
    for device, mine in sources:

        @pl.when(jnp.logical_not(mine))
        def _():
            pl.semaphore_signal(barrier, inc=1, device_id=device, device_id_type=MESH)

    def copy(src, dst, slot, device):
        return pltpu.make_async_remote_copy(
            src_ref=src, dst_ref=dst, send_sem=send_sem.at[slot], recv_sem=recv_sem.at[slot],
            device_id=device, device_id_type=MESH,
        )

    w_cols, p_cols = pl.ds(kt, ks), pl.ds(0, kt)

    def weight_copy(k, plane):
        return pltpu.make_async_remote_copy(
            src_ref=wt_ref.at[(n + k) % 4], dst_ref=ct.at[w_slab, rows, w_cols], send_sem=send_sem.at[WEIGHT + k],
            recv_sem=recv_sem.at[WEIGHT + plane], device_id=n_dev[k], device_id_type=MESH,
        )

    ct[w, rows, p_cols] = pt_ref[rows, :]

    @pl.when(holder)
    def _():
        fetch.wait()
        row = lax.broadcasted_iota(jnp.int32, (half, 256), 0)
        lane = lax.broadcasted_iota(jnp.int32, (half, 256), 1)
        pick = jnp.where(lane == row + (column - low), 1.0, 0.0).astype(BF16)

        def transpose(q, carry):
            span = pl.ds(pl.multiple_of(ks * q, ks), ks)
            wt_ref[q] = lax.dot_general(
                pick, window[span, :], (((1,), (1,)), ((), ())), preferred_element_type=F32
            ).astype(BF16)
            return carry

        lax.fori_loop(0, 4, transpose, 0)
        ct[w_slab, rows, w_cols] = wt_ref[n]

    eye = lax.broadcasted_iota(jnp.int32, (128, 128), 0) == lax.broadcasted_iota(jnp.int32, (128, 128), 1)
    groups = tokens // 128
    sq[0] = jnp.zeros((8, 128), F32)

    def squares(i, carry):
        part_t = t_ref[pl.ds(pl.multiple_of(128 * i, 128), 128), :].astype(F32)
        col = jnp.sum(part_t * part_t, axis=1, keepdims=True)
        sq[0, pl.ds(i, 1), :] = jnp.sum(jnp.where(eye, col, 0.0), axis=0, keepdims=True)
        return carry

    lax.fori_loop(0, groups, squares, 0)
    pl.semaphore_wait(barrier, jnp.where(at_home, len(greeted) + 18, len(greeted) + 19))

    z_copy = copy(ct.at[w, rows, p_cols], ct.at[w, rows, p_cols], ZSWAP, z_other)
    z_copy.start()

    @pl.when(holder)
    def _():
        for k in (2, 1, 3):
            weight_copy(k, n // 2).start()

    def weight_arrives(plane):
        @pl.when(n != 2 * plane + y // 2)
        def _():
            weight_copy(1, plane).wait_recv()

        @pl.when(zl != plane)
        def _():
            z_copy.wait_recv()

    def slab(index, part=None):
        if part is None:
            return ct.at[index, rows]
        return ct.at[index, rows, pl.ds(0, cut) if part == 0 else pl.ds(cut, depth - cut)]

    def spread(index, slot, device, part=None):
        return copy(slab(index, part), slab(index, part), slot, device)

    def start(item):
        item.start()

    along_a, along_b = jnp.where(c == 0, x, y), jnp.where(c == 0, y, x)

    def cell(plane, da, db):
        a, b = (along_a + da) % 4, (along_b + db) % 4
        return plane * 16 + jnp.where(c == 0, 4 * b + a, 4 * a + b)

    first = [{"wide": cell(zl, 1, 0)}, {"wide": cell(zl, 3, 0)}, {"wide": cell(zl, 2, 0)}]
    second = [{"wide": cell(zl, 0, 1)}, {"wide": cell(zl, 0, 3)}]
    ALONG = (0, 3, 1, 2)

    class Plane:
        def __init__(self, p, plane):
            self.base, self.p, self.plane = GATHER + 20 * p, p, plane

        def to_sibling(self, index):
            copy(slab(index), slab(index), SIBLING + self.p, sibling).start()

        def whole(self):
            planes = ct.at[pl.ds(16 * self.plane, 16), rows]
            return copy(planes, planes, SIBLING + self.p, sibling)

        def begin(self):
            weight_arrives(self.plane)
            own = cell(self.plane, 0, 0)
            for side in range(3):
                start(spread(own, self.base + side, first[side]))
            self.second_send(0)
            self.to_sibling(own)

        def second_send(self, j):
            index = cell(self.plane, ALONG[j], 0)
            for side in range(2):
                start(spread(index, self.base + 4 + 4 * j + side, second[side]))

        def first_near(self):
            for side in range(2):
                index = cell(self.plane, ALONG[1 + side], 0)
                spread(index, self.base + side, first[side]).wait_recv()
                self.second_send(1 + side)
                self.to_sibling(index)

        def first_far(self):
            index = cell(self.plane, 2, 0)
            spread(index, self.base + 2, first[2]).wait_recv()
            self.second_send(3)
            self.to_sibling(index)

        def second_near(self, j):
            slot = self.base + 4 + 4 * j
            for side in range(2):
                index = cell(self.plane, ALONG[j], 3 if side == 0 else 1)
                spread(index, slot + side, second[side]).wait_recv()
                start(spread(index, slot + 2 + side, second[side], side))
                self.to_sibling(index)

        def second_far(self, j):
            slot = self.base + 4 + 4 * j
            index = cell(self.plane, ALONG[j], 2)
            for side in range(2):
                spread(index, slot + 2 + side, second[side], side).wait_recv()
            self.to_sibling(index)

        def wait_sends(self):
            for side in range(3):
                spread(0, self.base + side, first[0]).wait_send()
            for j in range(4):
                for side in range(2):
                    spread(0, self.base + 4 + 4 * j + side, first[0]).wait_send()
                    spread(0, self.base + 6 + 4 * j + side, first[0], side).wait_send()

    p_first = 1 - n // 2
    near_plane, far_plane = Plane(0, p_first), Plane(1, 1 - p_first)
    near_plane.begin()

    sq_copies = [copy(sq.at[0], sq.at[d], SQUARES + d - 1, n_dev[d]) for d in (1, 2, 3)]
    for item in sq_copies:
        item.start()

    for item in sq_copies:
        item.wait_recv()
    inverse[...] = lax.rsqrt((sq[0] + sq[1] + sq[2] + sq[3]) / (4 * kt) + 1e-05)

    def normalize(i, carry):
        span = pl.ds(pl.multiple_of(128 * i, 128), 128)
        col = jnp.sum(jnp.where(eye, inverse[pl.ds(i, 1), :], 0.0), axis=1, keepdims=True)
        gain = g_ref[...].astype(F32).reshape(1, kt)
        hid[span, :] = -(t_ref[span, :].astype(F32) * col * gain).astype(BF16)
        lhs[span, pl.ds(kt, ks)] = x_ref[span, :]
        xt_ref[:, span] = x_ref[span, :].T
        return carry

    lax.fori_loop(0, groups, normalize, 0)
    paired_copy = copy(hid, lhs.at[:, pl.ds(0, kt)], PAIRED, sibling)
    paired_copy.start()

    near_plane.first_near()
    near_plane.second_near(0)
    near_plane.first_far()
    near_plane.second_near(1)
    near_plane.second_far(0)
    near_plane.second_near(2)
    near_plane.second_far(1)
    near_plane.second_near(3)
    far_plane.begin()
    far_plane.first_near()
    near_plane.second_far(2)
    near_plane.second_far(3)
    paired_copy.wait_recv()
    near_plane.whole().wait_recv()

    e2 = n % 2
    e1 = 1 - e2

    def by(e):
        return {"narrow": (n + 1 + 2 * e) % 4}

    def far_copy(e):
        return copy(far_out.at[e], far_in.at[e], NARROW_RS + e, by(e))

    def early_copy(e):
        return copy(near_out.at[e, 1 - e], near_in.at[e, 1 - e], NARROW_RS + 2 + e, by(e))

    def late_copy(e):
        return copy(near_out.at[e, e], near_in.at[e, e], NARROW_RS + 4 + e, by(e))

    def product(b, h):
        block = ct[pl.ds(8 * b + 4 * h, 4)].reshape(cols, depth)
        return lax.dot_general(lhs[...], block, (((1,), (1,)), ((), ())), preferred_element_type=F32)

    def send_late(e):
        far_copy(e).wait_recv()
        near_out[e, e] = (part[e] + far_in[e].astype(F32)).astype(BF16)
        late_copy(e).start()

    def products(i, carry):
        r, k = i // 2, i % 2

        @pl.when(i == 2)
        def _():
            far_plane.second_near(0)
            far_plane.first_far()

        @pl.when(i == 4)
        def _():
            far_plane.second_near(1)
            far_plane.second_far(0)
            far_plane.second_near(2)
            far_plane.second_far(1)
            far_plane.second_near(3)

        @pl.when(jnp.logical_or(i == 4, i == 6))
        def _():
            send_late(jnp.where(i == 4, e1, e2))

        @pl.when(i == 4)
        def _():
            far_plane.second_far(2)
            far_plane.second_far(3)
            far_plane.whole().wait_recv()

        e = jnp.where(r == 1, e1, e2)
        beside = jnp.logical_or(r == 1, r == 2)
        b = (n + jnp.where(r == 0, 2, jnp.where(r == 3, 0, 1 + 2 * e))) % 4
        h = jnp.where(beside, jnp.where(k == 0, 1 - e, e), k)
        early = jnp.logical_and(beside, k == 0)
        part[h] = product(b, h)

        @pl.when(r == 0)
        def _():
            far_out[k] = part[h].astype(BF16)
            far_copy(k).start()

        @pl.when(early)
        def _():
            near_out[e, h] = part[h].astype(BF16)
            early_copy(e).start()

        return carry

    lax.fori_loop(0, 8, products, 0)

    tiles = cols // 128

    def own_copy(h, e):
        return copy(m.at[n, h], m.at[n, h], NARROW_AG + 2 * e + h, by(e))

    def pass_on(e, j):
        piece = m.at[(n + 3 + 2 * e) % 4, e, j]
        return copy(piece, piece, NARROW_AG + 4 + tiles * e + j, by(e))

    def pass_all(e):
        def one(j, carry):
            pass_on(e, j).start()
            return carry

        lax.fori_loop(0, tiles, one, 0)

    def whole(b, h):
        return jnp.concatenate([m[b, h, j] for j in range(tiles)], axis=1)

    early_copy(e2).wait_recv()
    late_copy(e2).wait_recv()

    def finish(k, carry):
        h = jnp.where(k == 0, 1 - e1, e1)

        @pl.when(k == 0)
        def _():
            early_copy(e1).wait_recv()

        @pl.when(k == 1)
        def _():
            late_copy(e1).wait_recv()

        span = pl.ds(pl.multiple_of(cols * h, cols), cols)
        own = part[h] + x_ref[:, span].astype(F32)
        total = (own + near_in[0, h].astype(F32) + near_in[1, h].astype(F32)).astype(BF16)
        for j in range(tiles):
            m[n, h, j] = total[:, 128 * j : 128 * j + 128]
        own_copy(h, 0).start()
        own_copy(h, 1).start()
        return carry

    lax.fori_loop(0, 2, finish, 0)
    igacc[...] = jnp.zeros((tokens, ks), F32)
    me = 4 * y + x

    def core_copy(slot):
        return copy(core_out.at[slot], core_in.at[slot], CORE_SUM + slot, sibling)

    def core_tile(j):
        return copy(tile_out.at[j], tile_in.at[j], CORE_SUM + 3 + j, sibling)

    def wide_send(out, into, slot):
        def one(k, carry):
            yy, xx = peer(k)
            copy(out.at[4 * yy + xx], into.at[me], slot, {"wide": at(zl, yy, xx)}).start()
            return carry

        lax.fori_loop(1, 16, one, 0)

    def wide_all(out, into, slot):
        return copy(out.at[pl.ds(0, 15)], into.at[pl.ds(0, 15)], slot, {"wide": at(zl, y, (x + 1) % 4)})

    def wide_block(slot):
        return wide_all(wide_out.at[slot], wide_in.at[slot], WIDE_RS + slot)

    def wide_tile(j):
        return wide_all(far_wide_out.at[j], far_wide_in.at[j], WIDE_RS + 3 + j)

    def chip_sum(slot):
        core_copy(slot).wait_recv()
        both = (kept[...] + core_in[slot].astype(F32)).astype(BF16)
        wide_out[slot] = both.reshape(16, half, cols)
        wide_in[slot, me] = wide_out[slot, me]
        wide_send(wide_out.at[slot], wide_in.at[slot], WIDE_RS + slot)

    def final_copy(d):
        return pltpu.make_async_remote_copy(
            src_ref=fin_out.at[d], dst_ref=fin_in.at[zl, c], send_sem=send_sem.at[FINAL + d],
            recv_sem=recv_sem.at[FINAL + 2 * zl + c], device_id=target(d), device_id_type=MESH,
        )

    def reduce(slot):
        d = jnp.where(slot == 2, 3, slot)
        wide_block(slot).wait_recv()
        total = wide_in[slot, 0].astype(F32)
        for k in range(1, 16):
            total = total + wide_in[slot, k].astype(F32)
        stays = jnp.logical_and(at_home, d == 0)

        @pl.when(stays)
        def _():
            fin_in[zl, c] = total.astype(BF16)

        @pl.when(jnp.logical_not(stays))
        def _():
            fin_out[d] = total.astype(BF16)
            final_copy(d).start()

    def add_input_grad(b, h):
        block = ct[pl.ds(8 * b + 4 * h, 4), :, pl.ds(kt, ks)].reshape(cols, ks)
        igacc[...] += jnp.dot(whole(b, h), block, preferred_element_type=F32)

    soon = 1 - n % 2

    def backward(i, carry):
        @pl.when(jnp.logical_or(i == 2, i == 4))
        def _():
            arrived = jnp.where(i == 2, soon, 1 - soon)
            own_copy(arrived, arrived).wait_recv()
            pass_all(arrived)
            own_copy(arrived, 1 - arrived).wait_recv()

        d = jnp.where(i < 2, 0, jnp.where(i % 2 == 0, 3, 1))
        h = jnp.where(i == 0, 1 - c, jnp.where(i == 1, c, jnp.where(i < 4, soon, 1 - soon)))
        slot = jnp.where(d == 3, 2, d)
        b = (n + d) % 4
        kept[...] = jnp.dot(xt_ref[...], whole(b, h), preferred_element_type=F32)

        @pl.when(h != c)
        def _():
            core_out[slot] = kept[...].astype(BF16)
            core_copy(slot).start()

        add_input_grad(b, h)

        @pl.when(h == c)
        def _():
            chip_sum(slot)

        return carry

    def far_gradient(j, carry):
        b = (n + 2) % 4
        for e in range(2):
            pass_on(e, j).wait_recv()
        tile_out[j] = jnp.dot(xt_ref[...], m[b, 1 - c, j], preferred_element_type=F32).astype(BF16)
        core_tile(j).start()
        own = jnp.dot(xt_ref[...], m[b, c, j], preferred_element_type=F32)
        core_tile(j).wait_recv()
        far_wide_out[j] = (own + tile_in[j].astype(F32)).astype(BF16).reshape(16, half, 128)
        far_wide_in[j, me] = far_wide_out[j, me]
        wide_send(far_wide_out.at[j], far_wide_in.at[j], WIDE_RS + 3 + j)
        return carry

    def early_waits():
        for item in sq_copies + [z_copy, paired_copy, near_plane.whole(), far_plane.whole()]:
            item.wait_send()
        near_plane.wait_sends()
        far_plane.wait_sends()
        for e in range(2):
            far_copy(e).wait_send()
            early_copy(e).wait_send()
            late_copy(e).wait_send()

        @pl.when(holder)
        def _():
            for k in range(1, 4):
                weight_copy(k, n // 2).wait_send()

    def early_sums(slot, carry):
        reduce(slot)
        return carry

    def last_input_grad(h, carry):
        add_input_grad((n + 2) % 4, h)
        return carry

    lax.fori_loop(0, 6, backward, 0)
    early_waits()
    lax.fori_loop(0, tiles, far_gradient, 0)
    lax.fori_loop(0, 2, last_input_grad, 0)
    for h in range(2):
        span = slice(cols * h, cols * h + cols)
        ig_ref[:, span] = (whole(n, h).astype(F32) + igacc[:, span]).astype(BF16)

    lax.fori_loop(0, 3, early_sums, 0)
    for j in range(tiles):
        wide_tile(j).wait_recv()
        total = far_wide_in[j, 0].astype(F32)
        for k in range(1, 16):
            total = total + far_wide_in[j, k].astype(F32)
        fin_out[2, :, 128 * j : 128 * j + 128] = total.astype(BF16)
    final_copy(2).start()
    for e in range(2):
        for j in range(tiles):
            pass_on(e, j).wait_send()
        for h in range(2):
            own_copy(h, e).wait_send()
    for k in range(3):
        core_copy(k).wait_send()
        core_tile(k).wait_send()
        wide_block(k).wait_send()
        wide_tile(k).wait_send()

    def late_waits():
        for d in range(4):

            @pl.when(jnp.logical_not(jnp.logical_and(at_home, d == 0)))
            def _():
                final_copy(d).wait_send()

    scale = 1.0 / (tokens * 64.0) ** 0.5
    for zz in range(2):
        for cc in range(2):

            @pl.when(jnp.logical_not(sources[2 * zz + cc][1]))
            def _():
                pltpu.make_async_remote_copy(
                    src_ref=fin_out.at[0], dst_ref=fin_in.at[zz, cc], send_sem=send_sem.at[FINAL],
                    recv_sem=recv_sem.at[FINAL + 2 * zz + cc], device_id=sibling, device_id_type=MESH,
                ).wait_recv()

    for h in range(2):
        wg_ref[:, cols * h : cols * h + cols] = (fin_in[0, h].astype(F32) + fin_in[1, h].astype(F32)) * scale

    late_waits()


def shards(teacher_rows, teacher_gain, projector, student_rows, student_weight):
    tokens, kt = teacher_rows.shape
    ks = student_rows.shape[1]
    width = projector.shape[1]
    half, cols, depth = width // 2, ks // 2, kt + ks
    vmem = pl.BlockSpec(memory_space=pltpu.VMEM)
    return pl.pallas_call(
        kernel,
        out_shape=(
            jax.ShapeDtypeStruct((tokens, ks), BF16),
            jax.ShapeDtypeStruct((half, ks), F32),
        ),
        in_specs=[vmem] * 4 + [pl.BlockSpec(memory_space=pl.ANY)],
        out_specs=(vmem, vmem),
        scratch_shapes=[
            pltpu.VMEM((4 * ks, 256), BF16),
            pltpu.VMEM((4, half, ks), BF16),
            pltpu.VMEM((ks, tokens), BF16),
            pltpu.VMEM((32, width, depth), BF16),
            pltpu.VMEM((tokens, depth), BF16),
            pltpu.VMEM((tokens, kt), BF16),
            pltpu.VMEM((4, 8, 128), F32),
            pltpu.VMEM((8, 128), F32),
            pltpu.VMEM((2, tokens, cols), F32),
            pltpu.VMEM((2, tokens, cols), BF16),
            pltpu.VMEM((2, 2, tokens, cols), BF16),
            pltpu.VMEM((2, tokens, cols), BF16),
            pltpu.VMEM((2, 2, tokens, cols), BF16),
            pltpu.VMEM((4, 2, cols // 128, tokens, 128), BF16),
            pltpu.VMEM((tokens, ks), F32),
            pltpu.VMEM((ks, cols), F32),
            pltpu.VMEM((3, ks, cols), BF16),
            pltpu.VMEM((3, ks, cols), BF16),
            pltpu.VMEM((3, 16, half, cols), BF16),
            pltpu.VMEM((3, 16, half, cols), BF16),
            pltpu.VMEM((3, ks, 128), BF16),
            pltpu.VMEM((3, ks, 128), BF16),
            pltpu.VMEM((3, 16, half, 128), BF16),
            pltpu.VMEM((3, 16, half, 128), BF16),
            pltpu.VMEM((4, half, cols), BF16),
            pltpu.VMEM((2, 2, half, cols), BF16),
            pltpu.SemaphoreType.DMA((SLOTS,)),
            pltpu.SemaphoreType.DMA((SLOTS,)),
            pltpu.SemaphoreType.DMA,
        ],
        compiler_params=pltpu.CompilerParams(
            collective_id=0, has_side_effects=True, vmem_limit_bytes=60 * 2**20
        ),
    )(
        teacher_rows,
        teacher_gain,
        projector.T,
        student_rows,
        student_weight,
    )


def solution(mesh):
    placed = (
        P(("section", "wide"), "narrow"),
        P("narrow"),
        P("narrow", "wide"),
        P(("section", "wide"), "narrow"),
        P(None, "narrow"),
    )
    return jax.shard_map(
        shards,
        mesh=mesh,
        in_specs=placed,
        out_specs=(P(("section", "wide"), "narrow"), P(("section", "wide"), "narrow")),
        check_vma=False,
    )
```

```python
import functools

import jax
import jax.numpy as jnp
from jax import lax
from jax.experimental import pallas as pl
from jax.experimental.pallas import tpu as pltpu
from jax.sharding import PartitionSpec as P

MESH = pl.DeviceIdType.MESH
F32 = jnp.float32
BF16 = jnp.bfloat16

GATHER = 0
ZSWAP = 40
WEIGHT = 41
SQUARES = 45
PAIRED = 48
SIBLING = 49
NARROW_RS = 51
NARROW_AG = 57
CORE_SUM = 67
WIDE_RS = 73
FINAL = 79
SLOTS = 83


def kernel(
    t_ref, g_ref, pt_ref, x_ref, weight_ref, ig_ref, wg_ref, window, wt_ref, xt_ref,
    ct, lhs, hid, sq, inverse, part, far_out, near_out, far_in, near_in, m, igacc,
    kept, core_out, core_in, wide_out, wide_in, tile_out, tile_in, far_wide_out, far_wide_in, fin_out, fin_in, send_sem, recv_sem, local_sem,
):
    c = lax.axis_index("section")
    w = lax.axis_index("wide")
    n = lax.axis_index("narrow")
    x, y, zl = w % 4, (w // 4) % 4, w // 16
    tokens, kt = t_ref.shape
    ks = x_ref.shape[1]
    half = pt_ref.shape[0] // 2
    depth = kt + ks
    cut = (depth // 256 + 1) * 128
    cols = ks // 2
    rows = pl.ds(pl.multiple_of(half * c, half), half)

    def at(zz, yy, xx):
        return zz * 16 + yy * 4 + xx

    sibling = {"section": 1 - c}
    z_other = {"wide": at(1 - zl, y, x)}
    n_dev = [None] + [{"narrow": (n + d) % 4} for d in (1, 2, 3)]

    def peer(k):
        return (y + k // 4) % 4, (x + k % 4) % 4

    def target(d):
        return {"section": n // 2, "wide": at(n % 2, y, x), "narrow": (n + d) % 4}

    at_home = n == 2 * c + zl
    sources = [
        ({"section": cc, "wide": at(zz, y, x), "narrow": 2 * c + zl}, jnp.logical_and(at_home, jnp.logical_and(cc == c, zz == zl)))
        for zz in range(2)
        for cc in range(2)
    ]

    holder = n % 2 == y // 2
    w_slab = at(n // 2, y, x)
    column = 2 * half * (w % 8) + half * c
    low = jnp.minimum(column // 128 * 128, ks - 256)
    fetch = pltpu.make_async_copy(weight_ref.at[:, pl.ds(pl.multiple_of(low, 128), 256)], window, local_sem)

    @pl.when(holder)
    def _():
        fetch.start()

    barrier = pltpu.get_barrier_semaphore()
    greeted = [sibling, z_other, n_dev[1], n_dev[2], n_dev[3]]
    for device in greeted:
        pl.semaphore_signal(barrier, inc=1, device_id=device, device_id_type=MESH)

    def greet(k, carry):
        yy, xx = peer(k)
        pl.semaphore_signal(barrier, inc=1, device_id={"wide": at(zl, yy, xx)}, device_id_type=MESH)
        return carry

    lax.fori_loop(1, 16, greet, 0)
    for device, mine in sources:

        @pl.when(jnp.logical_not(mine))
        def _():
            pl.semaphore_signal(barrier, inc=1, device_id=device, device_id_type=MESH)

    def copy(src, dst, slot, device):
        return pltpu.make_async_remote_copy(
            src_ref=src, dst_ref=dst, send_sem=send_sem.at[slot], recv_sem=recv_sem.at[slot],
            device_id=device, device_id_type=MESH,
        )

    w_cols, p_cols = pl.ds(kt, ks), pl.ds(0, kt)

    def weight_copy(k, plane):
        return pltpu.make_async_remote_copy(
            src_ref=wt_ref.at[(n + k) % 4], dst_ref=ct.at[w_slab, rows, w_cols], send_sem=send_sem.at[WEIGHT + k],
            recv_sem=recv_sem.at[WEIGHT + plane], device_id=n_dev[k], device_id_type=MESH,
        )

    ct[w, rows, p_cols] = pt_ref[rows, :]

    @pl.when(holder)
    def _():
        fetch.wait()
        row = lax.broadcasted_iota(jnp.int32, (half, 256), 0)
        lane = lax.broadcasted_iota(jnp.int32, (half, 256), 1)
        pick = jnp.where(lane == row + (column - low), 1.0, 0.0).astype(BF16)

        def transpose(q, carry):
            span = pl.ds(pl.multiple_of(ks * q, ks), ks)
            wt_ref[q] = lax.dot_general(
                pick, window[span, :], (((1,), (1,)), ((), ())), preferred_element_type=F32
            ).astype(BF16)
            return carry

        lax.fori_loop(0, 4, transpose, 0)
        ct[w_slab, rows, w_cols] = wt_ref[n]

    eye = lax.broadcasted_iota(jnp.int32, (128, 128), 0) == lax.broadcasted_iota(jnp.int32, (128, 128), 1)
    groups = tokens // 128
    sq[0] = jnp.zeros((8, 128), F32)

    def squares(i, carry):
        part_t = t_ref[pl.ds(pl.multiple_of(128 * i, 128), 128), :].astype(F32)
        col = jnp.sum(part_t * part_t, axis=1, keepdims=True)
        sq[0, pl.ds(i, 1), :] = jnp.sum(jnp.where(eye, col, 0.0), axis=0, keepdims=True)
        return carry

    lax.fori_loop(0, groups, squares, 0)
    pl.semaphore_wait(barrier, jnp.where(at_home, len(greeted) + 18, len(greeted) + 19))

    z_copy = copy(ct.at[w, rows, p_cols], ct.at[w, rows, p_cols], ZSWAP, z_other)
    z_copy.start()

    @pl.when(holder)
    def _():
        for k in (2, 1, 3):
            weight_copy(k, n // 2).start()

    def weight_arrives(plane):
        @pl.when(n != 2 * plane + y // 2)
        def _():
            weight_copy(1, plane).wait_recv()

        @pl.when(zl != plane)
        def _():
            z_copy.wait_recv()

    def slab(index, part=None):
        if part is None:
            return ct.at[index, rows]
        return ct.at[index, rows, pl.ds(0, cut) if part == 0 else pl.ds(cut, depth - cut)]

    def spread(index, slot, device, part=None):
        return copy(slab(index, part), slab(index, part), slot, device)

    def start(item):
        item.start()

    along_a, along_b = jnp.where(c == 0, x, y), jnp.where(c == 0, y, x)

    def cell(plane, da, db):
        a, b = (along_a + da) % 4, (along_b + db) % 4
        return plane * 16 + jnp.where(c == 0, 4 * b + a, 4 * a + b)

    first = [{"wide": cell(zl, 1, 0)}, {"wide": cell(zl, 3, 0)}, {"wide": cell(zl, 2, 0)}]
    second = [{"wide": cell(zl, 0, 1)}, {"wide": cell(zl, 0, 3)}]
    ALONG = (0, 3, 1, 2)

    class Plane:
        def __init__(self, p, plane):
            self.base, self.p, self.plane = GATHER + 20 * p, p, plane

        def to_sibling(self, index):
            copy(slab(index), slab(index), SIBLING + self.p, sibling).start()

        def whole(self):
            planes = ct.at[pl.ds(16 * self.plane, 16), rows]
            return copy(planes, planes, SIBLING + self.p, sibling)

        def begin(self):
            weight_arrives(self.plane)
            own = cell(self.plane, 0, 0)
            for side in range(3):
                start(spread(own, self.base + side, first[side]))
            self.second_send(0)
            self.to_sibling(own)

        def second_send(self, j):
            index = cell(self.plane, ALONG[j], 0)
            for side in range(2):
                start(spread(index, self.base + 4 + 4 * j + side, second[side]))

        def first_near(self):
            for side in range(2):
                index = cell(self.plane, ALONG[1 + side], 0)
                spread(index, self.base + side, first[side]).wait_recv()
                self.second_send(1 + side)
                self.to_sibling(index)

        def first_far(self):
            index = cell(self.plane, 2, 0)
            spread(index, self.base + 2, first[2]).wait_recv()
            self.second_send(3)
            self.to_sibling(index)

        def second_near(self, j):
            slot = self.base + 4 + 4 * j
            for side in range(2):
                index = cell(self.plane, ALONG[j], 3 if side == 0 else 1)
                spread(index, slot + side, second[side]).wait_recv()
                start(spread(index, slot + 2 + side, second[side], side))
                self.to_sibling(index)

        def second_far(self, j):
            slot = self.base + 4 + 4 * j
            index = cell(self.plane, ALONG[j], 2)
            for side in range(2):
                spread(index, slot + 2 + side, second[side], side).wait_recv()
            self.to_sibling(index)

        def wait_sends(self):
            for side in range(3):
                spread(0, self.base + side, first[0]).wait_send()
            for j in range(4):
                for side in range(2):
                    spread(0, self.base + 4 + 4 * j + side, first[0]).wait_send()
                    spread(0, self.base + 6 + 4 * j + side, first[0], side).wait_send()

    p_first = 1 - n // 2
    near_plane, far_plane = Plane(0, p_first), Plane(1, 1 - p_first)
    near_plane.begin()

    sq_copies = [copy(sq.at[0], sq.at[d], SQUARES + d - 1, n_dev[d]) for d in (1, 2, 3)]
    for item in sq_copies:
        item.start()

    for item in sq_copies:
        item.wait_recv()
    inverse[...] = lax.rsqrt((sq[0] + sq[1] + sq[2] + sq[3]) / (4 * kt) + 1e-05)

    def normalize(i, carry):
        span = pl.ds(pl.multiple_of(128 * i, 128), 128)
        col = jnp.sum(jnp.where(eye, inverse[pl.ds(i, 1), :], 0.0), axis=1, keepdims=True)
        gain = g_ref[...].astype(F32).reshape(1, kt)
        hid[span, :] = -(t_ref[span, :].astype(F32) * col * gain).astype(BF16)
        lhs[span, pl.ds(kt, ks)] = x_ref[span, :]
        xt_ref[:, span] = x_ref[span, :].T
        return carry

    lax.fori_loop(0, groups, normalize, 0)
    paired_copy = copy(hid, lhs.at[:, pl.ds(0, kt)], PAIRED, sibling)
    paired_copy.start()

    near_plane.first_near()
    near_plane.second_near(0)
    near_plane.first_far()
    near_plane.second_near(1)
    near_plane.second_far(0)
    near_plane.second_near(2)
    near_plane.second_far(1)
    near_plane.second_near(3)
    far_plane.begin()
    far_plane.first_near()
    near_plane.second_far(2)
    near_plane.second_far(3)
    paired_copy.wait_recv()
    near_plane.whole().wait_recv()

    e2 = n % 2
    e1 = 1 - e2

    def by(e):
        return {"narrow": (n + 1 + 2 * e) % 4}

    def far_copy(e):
        return copy(far_out.at[e], far_in.at[e], NARROW_RS + e, by(e))

    def early_copy(e):
        return copy(near_out.at[e, 1 - e], near_in.at[e, 1 - e], NARROW_RS + 2 + e, by(e))

    def late_copy(e):
        return copy(near_out.at[e, e], near_in.at[e, e], NARROW_RS + 4 + e, by(e))

    def product(b, h):
        block = ct[pl.ds(8 * b + 4 * h, 4)].reshape(cols, depth)
        return lax.dot_general(lhs[...], block, (((1,), (1,)), ((), ())), preferred_element_type=F32)

    def send_late(e):
        far_copy(e).wait_recv()
        near_out[e, e] = (part[e] + far_in[e].astype(F32)).astype(BF16)
        late_copy(e).start()

    def products(i, carry):
        r, k = i // 2, i % 2

        @pl.when(i == 2)
        def _():
            far_plane.second_near(0)
            far_plane.first_far()

        @pl.when(i == 4)
        def _():
            far_plane.second_near(1)
            far_plane.second_far(0)
            far_plane.second_near(2)
            far_plane.second_far(1)
            far_plane.second_near(3)

        @pl.when(i == 4)
        def _():
            far_plane.second_far(2)
            far_plane.second_far(3)

        @pl.when(jnp.logical_or(i == 4, i == 6))
        def _():
            send_late(jnp.where(i == 4, e1, e2))

        @pl.when(i == 4)
        def _():
            far_plane.whole().wait_recv()

        e = jnp.where(r == 1, e1, e2)
        beside = jnp.logical_or(r == 1, r == 2)
        b = (n + jnp.where(r == 0, 2, jnp.where(r == 3, 0, 1 + 2 * e))) % 4
        h = jnp.where(beside, jnp.where(k == 0, 1 - e, e), k)
        early = jnp.logical_and(beside, k == 0)
        part[h] = product(b, h)

        @pl.when(r == 0)
        def _():
            far_out[k] = part[h].astype(BF16)
            far_copy(k).start()

        @pl.when(early)
        def _():
            near_out[e, h] = part[h].astype(BF16)
            early_copy(e).start()

        return carry

    lax.fori_loop(0, 8, products, 0)

    tiles = cols // 128

    def own_copy(h, e):
        return copy(m.at[n, h], m.at[n, h], NARROW_AG + 2 * e + h, by(e))

    def pass_on(e, j):
        piece = m.at[(n + 3 + 2 * e) % 4, e, j]
        return copy(piece, piece, NARROW_AG + 4 + tiles * e + j, by(e))

    def pass_all(e):
        def one(j, carry):
            pass_on(e, j).start()
            return carry

        lax.fori_loop(0, tiles, one, 0)

    def whole(b, h):
        return jnp.concatenate([m[b, h, j] for j in range(tiles)], axis=1)

    early_copy(e2).wait_recv()
    late_copy(e2).wait_recv()

    def finish(k, carry):
        h = jnp.where(k == 0, 1 - e1, e1)

        @pl.when(k == 0)
        def _():
            early_copy(e1).wait_recv()

        @pl.when(k == 1)
        def _():
            late_copy(e1).wait_recv()

        span = pl.ds(pl.multiple_of(cols * h, cols), cols)
        own = part[h] + x_ref[:, span].astype(F32)
        total = (own + near_in[0, h].astype(F32) + near_in[1, h].astype(F32)).astype(BF16)
        for j in range(tiles):
            m[n, h, j] = total[:, 128 * j : 128 * j + 128]
        own_copy(h, 0).start()
        own_copy(h, 1).start()
        return carry

    lax.fori_loop(0, 2, finish, 0)
    igacc[...] = jnp.zeros((tokens, ks), F32)
    me = 4 * y + x

    def core_copy(slot):
        return copy(core_out.at[slot], core_in.at[slot], CORE_SUM + slot, sibling)

    def core_tile(j):
        return copy(tile_out.at[j], tile_in.at[j], CORE_SUM + 3 + j, sibling)

    def wide_send(out, into, slot):
        def one(k, carry):
            yy, xx = peer(k)
            copy(out.at[4 * yy + xx], into.at[me], slot, {"wide": at(zl, yy, xx)}).start()
            return carry

        lax.fori_loop(1, 16, one, 0)

    def wide_all(out, into, slot):
        return copy(out.at[pl.ds(0, 15)], into.at[pl.ds(0, 15)], slot, {"wide": at(zl, y, (x + 1) % 4)})

    def wide_block(slot):
        return wide_all(wide_out.at[slot], wide_in.at[slot], WIDE_RS + slot)

    def wide_tile(j):
        return wide_all(far_wide_out.at[j], far_wide_in.at[j], WIDE_RS + 3 + j)

    def chip_sum(slot):
        core_copy(slot).wait_recv()
        both = (kept[...] + core_in[slot].astype(F32)).astype(BF16)
        wide_out[slot] = both.reshape(16, half, cols)
        wide_in[slot, me] = wide_out[slot, me]
        wide_send(wide_out.at[slot], wide_in.at[slot], WIDE_RS + slot)

    def final_copy(d):
        return pltpu.make_async_remote_copy(
            src_ref=fin_out.at[d], dst_ref=fin_in.at[zl, c], send_sem=send_sem.at[FINAL + d],
            recv_sem=recv_sem.at[FINAL + 2 * zl + c], device_id=target(d), device_id_type=MESH,
        )

    def reduce(slot):
        d = jnp.where(slot == 2, 3, slot)
        wide_block(slot).wait_recv()
        total = wide_in[slot, 0].astype(F32)
        for k in range(1, 16):
            total = total + wide_in[slot, k].astype(F32)
        stays = jnp.logical_and(at_home, d == 0)

        @pl.when(stays)
        def _():
            fin_in[zl, c] = total.astype(BF16)

        @pl.when(jnp.logical_not(stays))
        def _():
            fin_out[d] = total.astype(BF16)
            final_copy(d).start()

    def add_input_grad(b, h):
        block = ct[pl.ds(8 * b + 4 * h, 4), :, pl.ds(kt, ks)].reshape(cols, ks)
        igacc[...] += jnp.dot(whole(b, h), block, preferred_element_type=F32)

    soon = 1 - n % 2

    def backward(i, carry):
        @pl.when(jnp.logical_or(i == 2, i == 4))
        def _():
            arrived = jnp.where(i == 2, soon, 1 - soon)
            own_copy(arrived, arrived).wait_recv()
            pass_all(arrived)
            own_copy(arrived, 1 - arrived).wait_recv()

        d = jnp.where(i < 2, 0, jnp.where(i % 2 == 0, 3, 1))
        h = jnp.where(i == 0, 1 - c, jnp.where(i == 1, c, jnp.where(i < 4, soon, 1 - soon)))
        slot = jnp.where(d == 3, 2, d)
        b = (n + d) % 4
        kept[...] = jnp.dot(xt_ref[...], whole(b, h), preferred_element_type=F32)

        @pl.when(h != c)
        def _():
            core_out[slot] = kept[...].astype(BF16)
            core_copy(slot).start()

        add_input_grad(b, h)

        @pl.when(h == c)
        def _():
            chip_sum(slot)

        return carry

    def far_gradient(j, carry):
        b = (n + 2) % 4
        for e in range(2):
            pass_on(e, j).wait_recv()
        tile_out[j] = jnp.dot(xt_ref[...], m[b, 1 - c, j], preferred_element_type=F32).astype(BF16)
        core_tile(j).start()
        own = jnp.dot(xt_ref[...], m[b, c, j], preferred_element_type=F32)
        core_tile(j).wait_recv()
        far_wide_out[j] = (own + tile_in[j].astype(F32)).astype(BF16).reshape(16, half, 128)
        far_wide_in[j, me] = far_wide_out[j, me]
        wide_send(far_wide_out.at[j], far_wide_in.at[j], WIDE_RS + 3 + j)
        return carry

    def early_waits():
        for item in sq_copies + [z_copy, paired_copy, near_plane.whole(), far_plane.whole()]:
            item.wait_send()
        near_plane.wait_sends()
        far_plane.wait_sends()
        for e in range(2):
            far_copy(e).wait_send()
            early_copy(e).wait_send()
            late_copy(e).wait_send()

        @pl.when(holder)
        def _():
            for k in range(1, 4):
                weight_copy(k, n // 2).wait_send()

    def early_sums(slot, carry):
        reduce(slot)
        return carry

    def last_input_grad(h, carry):
        add_input_grad((n + 2) % 4, h)
        return carry

    lax.fori_loop(0, 6, backward, 0)
    early_waits()
    lax.fori_loop(0, tiles, far_gradient, 0)
    lax.fori_loop(0, 2, last_input_grad, 0)
    for h in range(2):
        span = slice(cols * h, cols * h + cols)
        ig_ref[:, span] = (whole(n, h).astype(F32) + igacc[:, span]).astype(BF16)

    lax.fori_loop(0, 3, early_sums, 0)
    for j in range(tiles):
        wide_tile(j).wait_recv()
        total = far_wide_in[j, 0].astype(F32)
        for k in range(1, 16):
            total = total + far_wide_in[j, k].astype(F32)
        fin_out[2, :, 128 * j : 128 * j + 128] = total.astype(BF16)
    final_copy(2).start()
    for e in range(2):
        for j in range(tiles):
            pass_on(e, j).wait_send()
        for h in range(2):
            own_copy(h, e).wait_send()
    for k in range(3):
        core_copy(k).wait_send()
        core_tile(k).wait_send()
        wide_block(k).wait_send()
        wide_tile(k).wait_send()

    def late_waits():
        for d in range(4):

            @pl.when(jnp.logical_not(jnp.logical_and(at_home, d == 0)))
            def _():
                final_copy(d).wait_send()

    scale = 1.0 / (tokens * 64.0) ** 0.5
    for zz in range(2):
        for cc in range(2):

            @pl.when(jnp.logical_not(sources[2 * zz + cc][1]))
            def _():
                pltpu.make_async_remote_copy(
                    src_ref=fin_out.at[0], dst_ref=fin_in.at[zz, cc], send_sem=send_sem.at[FINAL],
                    recv_sem=recv_sem.at[FINAL + 2 * zz + cc], device_id=sibling, device_id_type=MESH,
                ).wait_recv()

    for h in range(2):
        wg_ref[:, cols * h : cols * h + cols] = (fin_in[0, h].astype(F32) + fin_in[1, h].astype(F32)) * scale

    late_waits()


def shards(teacher_rows, teacher_gain, projector, student_rows, student_weight):
    tokens, kt = teacher_rows.shape
    ks = student_rows.shape[1]
    width = projector.shape[1]
    half, cols, depth = width // 2, ks // 2, kt + ks
    vmem = pl.BlockSpec(memory_space=pltpu.VMEM)
    return pl.pallas_call(
        kernel,
        out_shape=(
            jax.ShapeDtypeStruct((tokens, ks), BF16),
            jax.ShapeDtypeStruct((half, ks), F32),
        ),
        in_specs=[vmem] * 4 + [pl.BlockSpec(memory_space=pl.ANY)],
        out_specs=(vmem, vmem),
        scratch_shapes=[
            pltpu.VMEM((4 * ks, 256), BF16),
            pltpu.VMEM((4, half, ks), BF16),
            pltpu.VMEM((ks, tokens), BF16),
            pltpu.VMEM((32, width, depth), BF16),
            pltpu.VMEM((tokens, depth), BF16),
            pltpu.VMEM((tokens, kt), BF16),
            pltpu.VMEM((4, 8, 128), F32),
            pltpu.VMEM((8, 128), F32),
            pltpu.VMEM((2, tokens, cols), F32),
            pltpu.VMEM((2, tokens, cols), BF16),
            pltpu.VMEM((2, 2, tokens, cols), BF16),
            pltpu.VMEM((2, tokens, cols), BF16),
            pltpu.VMEM((2, 2, tokens, cols), BF16),
            pltpu.VMEM((4, 2, cols // 128, tokens, 128), BF16),
            pltpu.VMEM((tokens, ks), F32),
            pltpu.VMEM((ks, cols), F32),
            pltpu.VMEM((3, ks, cols), BF16),
            pltpu.VMEM((3, ks, cols), BF16),
            pltpu.VMEM((3, 16, half, cols), BF16),
            pltpu.VMEM((3, 16, half, cols), BF16),
            pltpu.VMEM((3, ks, 128), BF16),
            pltpu.VMEM((3, ks, 128), BF16),
            pltpu.VMEM((3, 16, half, 128), BF16),
            pltpu.VMEM((3, 16, half, 128), BF16),
            pltpu.VMEM((4, half, cols), BF16),
            pltpu.VMEM((2, 2, half, cols), BF16),
            pltpu.SemaphoreType.DMA((SLOTS,)),
            pltpu.SemaphoreType.DMA((SLOTS,)),
            pltpu.SemaphoreType.DMA,
        ],
        compiler_params=pltpu.CompilerParams(
            collective_id=0, has_side_effects=True, vmem_limit_bytes=60 * 2**20
        ),
    )(
        teacher_rows,
        teacher_gain,
        projector.T,
        student_rows,
        student_weight,
    )


def solution(mesh):
    placed = (
        P(("section", "wide"), "narrow"),
        P("narrow"),
        P("narrow", "wide"),
        P(("section", "wide"), "narrow"),
        P(None, "narrow"),
    )
    return jax.shard_map(
        shards,
        mesh=mesh,
        in_specs=placed,
        out_specs=(P(("section", "wide"), "narrow"), P(("section", "wide"), "narrow")),
        check_vma=False,
    )
```
